512 devices in a mesh: tm: 16 (over y, core), freq: 32 (over x, z).
Axes of the slice: x: 4, y: 8, z: 8, core: 2. Of those that a mesh axis runs over, the one named last changes fastest.
Arguments:
- emission: bfloat16 [16, 2, 1048576], P('tm', None, 'freq'), may hold values from 0.05 to 40, as said below
- step_weights: float32 [64, 3], replicated, may hold values from 0.2 to 5
- template_ids: int32 [2], replicated, may hold values from 0 to 63
Outputs:
- posterior: float32 [16, 2, 1048576], P('tm', None, 'freq')
- evidence: float32 [2], replicated
The draws below stay inside these ranges and needn't reach their ends.
Inputs may be any that keep to these rules, and one draw needn't show every extreme that they name: `emission`: every entry is positive.
All inputs are finite; a program needn't handle non-finite values.
Results may differ from the reference program's by a relative error of at most 0.0003.
Values sent between devices are 32-bit elements; how exact they have to be, the bound alone decides.
A program may use at most 64 MiB of HBM per device.

```python
import math
import jax
import jax.numpy as jnp
from jax import lax

BINS = 1048576
NTABLE = 64
TEMPL = 2
TIME = 16


def draw_emission(key, part):
    key = jax.random.fold_in(key, 7)
    shape = (TIME, TEMPL, BINS)
    position = jnp.arange(BINS, dtype=jnp.float32) / BINS
    ramp = jnp.exp(math.log(3.0) * position / TIME)
    noise = jnp.clip(jax.random.normal(key, shape, jnp.float32), -4.0, 4.0)
    values = jnp.exp(0.6 * noise) * ramp
    return values.astype(jnp.bfloat16)


def setup_inputs(seed: int = 0) -> dict:
    splits = jax.random.split(jax.random.key(seed), 4)
    return {
        "emission": draw_emission(jax.random.fold_in(splits[3], 71), 0),
        "step_weights": jnp.clip(jnp.exp(jax.random.uniform(splits[1], (NTABLE, 3), jnp.float32, math.log(0.2), math.log(5.0))), 0.2, 5.0),
        "template_ids": jax.random.randint(splits[2], (TEMPL,), 0, NTABLE).astype(jnp.int32),
    }


def advance(field, staying, rising, falling):
    padded = jnp.pad(field, ((0, 0), (1, 1)))
    return staying * field + rising * padded[:, :-2] + falling * padded[:, 2:]


def retreat(field, staying, rising, falling):
    padded = jnp.pad(field, ((0, 0), (1, 1)))
    return staying * field + rising * padded[:, 2:] + falling * padded[:, :-2]


def reference(emission, step_weights, template_ids):
    bank_rows = jnp.arange(NTABLE, dtype=jnp.int32)
    onehot = (template_ids[:, None] == bank_rows[None, :]).astype(jnp.float32)
    weights = jnp.dot(onehot, step_weights, precision=lax.Precision.HIGHEST, preferred_element_type=jnp.float32)
    chances = weights / jnp.sum(weights, axis=1, keepdims=True)
    staying, rising, falling = chances[:, 0:1], chances[:, 1:2], chances[:, 2:3]
    prior_mass = jnp.full((TEMPL, BINS), 1.0 / BINS, jnp.float32)

    def forward_step(previous, emission_row):
        updated = emission_row.astype(jnp.float32) * advance(previous, staying, rising, falling)
        totals = jnp.sum(updated, axis=1)
        normalized = updated / totals[:, None]
        return normalized, (normalized, jnp.log(totals))

    _, (alphas, log_totals) = lax.scan(forward_step, prior_mass, emission)

    closing_mass = jnp.full((TEMPL, BINS), 1.0 / BINS, jnp.float32)

    def backward_step(previous, emission_row):
        updated = retreat(emission_row.astype(jnp.float32) * previous, staying, rising, falling)
        normalized = updated / jnp.sum(updated, axis=1)[:, None]
        return normalized, normalized

    _, betas_early = lax.scan(backward_step, closing_mass, emission[1:], reverse=True)
    betas = jnp.concatenate([betas_early, closing_mass[None]], axis=0)
    joint_mass = alphas * betas
    posterior = BINS * joint_mass / jnp.sum(joint_mass, axis=2, keepdims=True)
    evidence = jnp.sum(log_totals, axis=0) / TIME
    return posterior, evidence
```

```python
import functools

import jax
import jax.numpy as jnp
from jax import lax
from jax.experimental import pallas as pl
from jax.experimental.pallas import tpu as pltpu
from jax.sharding import PartitionSpec as P

MESH = pl.DeviceIdType.MESH
Z_CHIPS = 8
LANES = 128
TAIL = 8


def ring_order(chips):
    steps = [chips // 2]
    for d in range(chips // 2 - 1, 0, -1):
        steps += [-d, d]
    return [(d, c) for d in steps for c in (0, 1)] + [(0, 1)]


def kernel(groups, freqs, zs, bins, x_hbm, w_hbm, ids_hbm, post_ref, level_ref,
           x_half, x_full, w_ref, ids_ref, stage, recv, halo, edge, beside, work,
           part, part_in, z_part, z_in, x_part, x_in, home, relay, relay_back,
           load_sem, send_sem, recv_sem, edge_send, edge_recv, halo_send, halo_recv, back_send, back_recv,
           part_send, part_recv, z_send, z_recv, x_send, x_recv, own_sem,
           relay_recv, pass_send):
    xs = freqs // zs
    chips = groups // 2
    tm = lax.axis_index("tm")
    fq = lax.axis_index("freq")
    yi = tm // 2
    core = lax.rem(tm, 2)
    xi = fq // zs
    zi = lax.rem(fq, zs)
    next_fq = lax.rem(fq + 1, freqs)
    prev_fq = lax.rem(fq + freqs - 1, freqs)
    all_rows = x_hbm.shape[0]
    rows = all_rows // groups
    last = groups - 1
    order = ring_order(chips)

    def member(k):
        return lax.rem(yi + k[0] + chips, chips) * 2 + lax.rem(core + k[1], 2)

    loads = [pltpu.make_async_copy(src, dst, load_sem.at[i])
             for i, (src, dst) in enumerate(((x_hbm, x_half), (w_hbm, w_ref), (ids_hbm, ids_ref)))]
    for copy in loads:
        copy.start()

    barrier = pltpu.get_barrier_semaphore()

    def greet(t, f):
        pl.semaphore_signal(barrier, inc=1, device_id=(t, f), device_id_type=MESH)

    def across_x(k):
        place = lax.rem(xi * 2 + core + k, 2 * xs)
        return place, (yi * 2 + lax.rem(place, 2), place // 2 * zs + zi)

    peers = [(min(abs(k[0]), chips - abs(k[0])), member(k), fq) for k in order]
    peers += [(min(k, zs - k), tm, xi * zs + lax.rem(zi + k, zs)) for k in range(1, zs)]
    peers += [(min(k // 2, xs - k // 2), *across_x(k)[1]) for k in range(1, 2 * xs)]
    for _, t, f in sorted(peers, key=lambda peer: -peer[0]):
        greet(t, f)
    has_next = fq < freqs - 1
    has_prev = fq > 0
    next_turns = has_next & (zi == zs - 1)
    prev_turns = has_prev & (zi == 0)
    low_halo = (yi == 0) & has_prev
    high_halo = (yi == chips - 1) & has_next

    @pl.when(next_turns)
    def _():
        greet(tm, next_fq)

    @pl.when(prev_turns)
    def _():
        greet(tm, prev_fq)

    loads[0].wait()
    for r in range(0, all_rows, 16):
        x_full[r:r + 16, :] = x_half[r:r + 16, :].astype(jnp.float32)
    low_lanes = lax.broadcasted_iota(jnp.int32, (1, LANES), 1) < LANES // 2
    nothing = jnp.zeros((1, LANES), jnp.float32)
    for o in range(chips):
        for p in range(2):
            first = 2 * o * rows + p
            for r in range(0, rows, 8):
                stage[2 * o + p, r:r + 8, :] = x_full[pl.ds(first + 2 * r, 8, stride=2), :]
            after = first + 2 * rows
            high = x_full[after:after + 1, :] if o < chips - 1 else nothing
            low = x_full[first - 2:first - 1, :] if o > 0 else nothing
            stage[2 * o + p, rows:rows + 1, :] = jnp.where(low_lanes, high, low)
    for p in range(2):
        edge[0, p] = x_full[all_rows - 2 + p:all_rows - 1 + p, :]
        edge[1, p] = x_full[p:p + 1, :]

    expected = (groups - 1) + (zs - 1) + (2 * xs - 1)
    pl.semaphore_wait(barrier, expected + next_turns.astype(jnp.int32) + prev_turns.astype(jnp.int32))

    def remote(src, dst, s_sem, r_sem, to):
        return pltpu.make_async_remote_copy(
            src_ref=src, dst_ref=dst, send_sem=s_sem, recv_sem=r_sem, device_id=to, device_id_type=MESH)

    def all_of(ref, count, sem):
        block = ref.at[pl.ds(0, count)]
        pltpu.make_async_copy(block, block, sem).wait()

    def out_copy(k):
        to = member(k)
        return remote(stage.at[to], recv.at[tm], send_sem.at[0], recv_sem.at[0], (to, fq))

    def edge_copy(side, to):
        return remote(edge.at[side], beside.at[side], edge_send.at[side], edge_recv.at[side], (tm, to))

    def halo_copy(side, p):
        owner = p if side == 0 else last - 1 + p
        to = jnp.where(tm == owner, owner + 1 - 2 * p, owner)
        return tm == owner, remote(
            beside.at[side, p], halo.at[tm], halo_send.at[side, p], halo_recv.at[0], (to, fq))

    def halo_pass(side):
        edge_copy(side, fq).wait_recv()
        for p in range(2):
            here, copy = halo_copy(side, p)

            @pl.when(here)
            def _():
                pltpu.make_async_copy(beside.at[side, p], halo.at[tm], halo_recv.at[0]).start()

            @pl.when(jnp.logical_not(here))
            def _():
                copy.start()

    def halo_sent(side):
        for p in range(2):
            here, copy = halo_copy(side, p)

            @pl.when(jnp.logical_not(here))
            def _():
                copy.wait_send()

    @pl.when(has_next)
    def _():
        edge_copy(0, next_fq).start()

    @pl.when(has_prev)
    def _():
        edge_copy(1, prev_fq).start()

    far = chips // 2
    near = far // 2
    direct = [k for k in order if k[0] != far]

    def relay_copy(src, dst, phase, c):
        way = near if c == 0 else -near
        return remote(src.at[member((far, lax.rem(core + c, 2)))], dst.at[c],
                      (send_sem, back_send)[phase].at[0], relay_recv.at[phase, c], (member((way, 0)), fq))

    def pass_copy(src, dst, r_sem, phase, c):
        way = near if c == 0 else -near
        origin = member((-way, 0))
        return remote(src.at[c], dst.at[origin], pass_send.at[phase], r_sem.at[0],
                      (member((way, lax.rem(core + c, 2))), fq))

    for c in (0, 1):
        relay_copy(stage, relay, 0, c).start()
    for k in direct:
        out_copy(k).start()

    @pl.when(has_prev)
    def _():
        halo_pass(0)

    @pl.when(has_next)
    def _():
        halo_pass(1)

    own = pltpu.make_async_copy(stage.at[tm], recv.at[tm], own_sem.at[0])
    own.start()

    for c in (0, 1):
        relay_copy(stage, relay, 0, c).wait_recv()
        pass_copy(relay, recv, recv_sem, 0, c).start()

    loads[1].wait()
    loads[2].wait()
    slot = lax.broadcasted_iota(jnp.int32, w_ref.shape, 1)
    weights = jnp.sum(jnp.where(slot == ids_ref[core], w_ref[...], 0.0), axis=1, keepdims=True)
    weights = weights / jnp.sum(weights, axis=0, keepdims=True)
    field = (rows + TAIL, LANES)
    staying, rising, falling = (jnp.broadcast_to(weights[i:i + 1, :], field) for i in range(3))
    lane = lax.broadcasted_iota(jnp.int32, field, 1)
    row_index = lax.broadcasted_iota(jnp.int32, field, 0)

    from_other = (high_halo & low_lanes) | (low_halo & jnp.logical_not(low_lanes))

    def emission_of(t):
        tail = jnp.where(from_other, halo[t], recv[t, rows:rows + 1, :])
        return jnp.concatenate([recv[t, 0:rows, :], jnp.broadcast_to(tail, (TAIL, LANES))], axis=0)

    def below(v):
        turned = pltpu.roll(v, 1, 1)
        return jnp.where(lane == 0, pltpu.roll(turned, 1, 0), turned)

    def above(v):
        turned = pltpu.roll(v, LANES - 1, 1)
        return jnp.where(lane == LANES - 1, pltpu.roll(turned, field[0] - 1, 0), turned)

    own.wait()
    all_of(recv, groups - 1, recv_sem.at[0])

    @pl.when(low_halo | high_halo)
    def _():
        all_of(halo, groups, halo_recv.at[0])

    world_low = (yi == 0) & (fq == 0)
    world_high = (yi == chips - 1) & (fq == freqs - 1)
    outside = ((row_index == rows) & world_high) | ((row_index > rows) & world_low)
    b = jnp.ones(field, jnp.float32)
    u = jnp.where(outside, 0.0, b)

    def forward(t, u):
        return emission_of(t) * (staying * u + rising * below(u) + falling * above(u))

    def backward(s, b):
        g = emission_of(s + 1) * b
        return staying * g + rising * above(g) + falling * below(g)

    half = groups // 2
    for step in range(half):
        u = forward(step, u)
        work[step] = u[:rows]
        if step > 0:
            b = backward(last - step, b)
        work[last - step] = b[:rows]
    b = backward(half - 1, b)
    middle = u[:rows] * b[:rows]
    work[half - 1] = middle
    part[...] = jnp.sum(middle, axis=0, keepdims=True)

    def spread(src, dst, to_of, mine, count, s_sem, r_sem):
        for k in range(1, count):
            remote(src, dst.at[mine], s_sem.at[0], r_sem.at[0], to_of(k)).start()

    def gather(src, dst, to_of, mine, count, s_sem, r_sem):
        all_of(dst, count - 1, r_sem.at[0])
        value = src[...]
        for k in range(1, count):
            value = value + dst[lax.rem(mine + k, count)]
        return value

    y_ring = (lambda k: (lax.rem(yi + k, chips) * 2 + core, fq), yi, chips, part_send, part_recv)
    z_ring = (lambda k: (tm, xi * zs + lax.rem(zi + k, zs)), zi, zs, z_send, z_recv)
    x_ring = (lambda k: across_x(k)[1], xi * 2 + core, 2 * xs, x_send, x_recv)
    spread(part, part_in, *y_ring)

    for step in range(half, groups):
        u = forward(step, u)
        work[step] = u[:rows] * work[step]
        if step > half:
            b = backward(last - step, b)
            work[last - step] = work[last - step] * b[:rows]

    def back_copy(k):
        to = member(k)
        return remote(work.at[to], home.at[tm], back_send.at[0], back_recv.at[0], (to, fq))

    own_back = pltpu.make_async_copy(work.at[tm], home.at[tm], own_sem.at[1])
    own_back.start()
    for c in (0, 1):
        relay_copy(work, relay_back, 1, c).start()
    for k in direct:
        back_copy(k).start()

    z_part[...] = gather(part, part_in, *y_ring)
    spread(z_part, z_in, *z_ring)
    for c in (0, 1):
        relay_copy(work, relay_back, 1, c).wait_recv()
        pass_copy(relay_back, home, back_recv, 1, c).start()
    all_of(stage, groups - 1, send_sem.at[0])
    all_of(relay, 2, pass_send.at[0])

    x_part[...] = gather(z_part, z_in, *z_ring)
    spread(x_part, x_in, *x_ring)

    @pl.when(has_next)
    def _():
        edge_copy(0, next_fq).wait_send()
        halo_sent(1)

    @pl.when(has_prev)
    def _():
        edge_copy(1, prev_fq).wait_send()
        halo_sent(0)

    all_of(part_in, chips - 1, part_send.at[0])
    all_of(z_in, zs - 1, z_send.at[0])
    all_of(x_in, 2 * xs - 1, x_recv.at[0])
    same = x_part[...]
    other = jnp.zeros_like(same)
    for k in range(1, 2 * xs):
        place, _ = across_x(k)
        if k % 2 == 0:
            same = same + x_in[place]
        else:
            other = other + x_in[place]
    totals = []
    for p in range(2):
        whole = jnp.sum(jnp.where(core == p, same, other), axis=1, keepdims=True)
        totals.append(whole)
        level_ref[p] = (jnp.log(whole * (1.0 / bins)) * (1.0 / groups))[0, 0]

    def settle(source):
        parity = lax.rem(source, 2)
        scale = bins / jnp.where(parity == 0, totals[0], totals[1])
        first_row = source // 2 * (2 * rows) + parity
        for r in range(0, rows, 8):
            post_ref[pl.ds(first_row + 2 * r, 8, stride=2), :] = home[source, r:r + 8, :] * scale

    own_back.wait()
    all_of(home, groups - 1, back_recv.at[0])
    settle(tm)
    for k in order:
        settle(member(k))
    all_of(x_in, 2 * xs - 1, x_send.at[0])
    all_of(work, groups - 1, back_send.at[0])
    all_of(relay_back, 2, pass_send.at[1])


def body(bins, groups, freqs, zs, emission, step_weights, template_ids):
    templates = emission.shape[1]
    here = emission.shape[2]
    total_rows = here // LANES
    all_rows = templates * total_rows
    rows = all_rows // groups
    xs = freqs // zs
    f32 = jnp.float32
    dma = pltpu.SemaphoreType.DMA
    lines = emission.reshape(templates, total_rows, LANES).transpose(1, 0, 2).reshape(all_rows, LANES)
    hbm = pl.BlockSpec(memory_space=pltpu.HBM)
    vmem = pl.BlockSpec(memory_space=pltpu.VMEM)
    post, level = pl.pallas_call(
        functools.partial(kernel, groups, freqs, zs, bins),
        out_shape=(
            jax.ShapeDtypeStruct((all_rows, LANES), f32),
            jax.ShapeDtypeStruct((templates,), f32),
        ),
        in_specs=[hbm, hbm, hbm],
        out_specs=(vmem, pl.BlockSpec(memory_space=pltpu.SMEM)),
        scratch_shapes=[
            pltpu.VMEM((all_rows, LANES), emission.dtype),
            pltpu.VMEM((all_rows, LANES), f32),
            pltpu.VMEM((step_weights.shape[1], step_weights.shape[0]), f32),
            pltpu.SMEM(template_ids.shape, jnp.int32),
            pltpu.VMEM((groups, rows + 1, LANES), f32),
            pltpu.VMEM((groups, rows + 1, LANES), f32),
            pltpu.VMEM((groups, 1, LANES), f32),
            pltpu.VMEM((2, 2, 1, LANES), f32),
            pltpu.VMEM((2, 2, 1, LANES), f32),
            pltpu.VMEM((groups, rows, LANES), f32),
            pltpu.VMEM((1, LANES), f32),
            pltpu.VMEM((groups // 2, 1, LANES), f32),
            pltpu.VMEM((1, LANES), f32),
            pltpu.VMEM((zs, 1, LANES), f32),
            pltpu.VMEM((1, LANES), f32),
            pltpu.VMEM((2 * xs, 1, LANES), f32),
            pltpu.VMEM((groups, rows, LANES), f32),
            pltpu.VMEM((2, rows + 1, LANES), f32),
            pltpu.VMEM((2, rows, LANES), f32),
            dma((3,)), dma((1,)), dma((1,)), dma((2,)), dma((2,)), dma((2, 2)), dma((1,)), dma((1,)), dma((1,)),
            dma((1,)), dma((1,)), dma((1,)), dma((1,)), dma((1,)), dma((1,)), dma((2,)),
            dma((2, 2)), dma((2,)),
        ],
        compiler_params=pltpu.CompilerParams(
            collective_id=0, has_side_effects=True, vmem_limit_bytes=32 * 1024 * 1024
        ),
    )(*(pltpu.with_memory_space_constraint(v, pltpu.HBM) for v in (lines, step_weights.T, template_ids)))
    posterior = post.reshape(total_rows, templates, LANES).transpose(1, 0, 2).reshape(1, templates, here)
    return posterior, level


def solution(mesh):
    groups, freqs = mesh.shape["tm"], mesh.shape["freq"]
    zs = min(Z_CHIPS, freqs // 2)

    def whole(emission, step_weights, template_ids):
        return jax.shard_map(
            functools.partial(body, emission.shape[2], groups, freqs, zs),
            mesh=mesh,
            in_specs=(P("tm", None, "freq"), P(), P()),
            out_specs=(P("tm", None, "freq"), P()),
            check_vma=False,
        )(emission, step_weights, template_ids)

    return whole
```

```python
import functools

import jax
import jax.numpy as jnp
from jax import lax
from jax.experimental import pallas as pl
from jax.experimental.pallas import tpu as pltpu
from jax.sharding import PartitionSpec as P

MESH = pl.DeviceIdType.MESH
Z_CHIPS = 8
LANES = 128
TAIL = 8


def ring_order(chips):
    steps = [chips // 2]
    for d in range(chips // 2 - 1, 0, -1):
        steps += [-d, d]
    return [(d, c) for d in steps for c in (0, 1)] + [(0, 1)]


def kernel(groups, freqs, zs, bins, x_hbm, w_hbm, ids_hbm, home, total_ref,
           x_half, x_full, w_ref, ids_ref, stage, recv, halo, edge, beside, work,
           part, part_in, z_part, z_in, x_part, x_in, relay, relay_back,
           load_sem, send_sem, recv_sem, edge_send, edge_recv, halo_send, halo_recv, back_send, back_recv,
           part_send, part_recv, z_send, z_recv, x_send, x_recv, own_sem,
           relay_recv, pass_send):
    xs = freqs // zs
    chips = groups // 2
    tm = lax.axis_index("tm")
    fq = lax.axis_index("freq")
    yi = tm // 2
    core = lax.rem(tm, 2)
    xi = fq // zs
    zi = lax.rem(fq, zs)
    next_fq = lax.rem(fq + 1, freqs)
    prev_fq = lax.rem(fq + freqs - 1, freqs)
    all_rows = x_hbm.shape[0]
    rows = all_rows // groups
    last = groups - 1
    order = ring_order(chips)

    def member(k):
        return lax.rem(yi + k[0] + chips, chips) * 2 + lax.rem(core + k[1], 2)

    loads = [pltpu.make_async_copy(src, dst, load_sem.at[i])
             for i, (src, dst) in enumerate(((x_hbm, x_half), (w_hbm, w_ref), (ids_hbm, ids_ref)))]
    for copy in loads:
        copy.start()

    barrier = pltpu.get_barrier_semaphore()

    def greet(t, f):
        pl.semaphore_signal(barrier, inc=1, device_id=(t, f), device_id_type=MESH)

    def across_x(k):
        place = lax.rem(xi * 2 + core + k, 2 * xs)
        return place, (yi * 2 + lax.rem(place, 2), place // 2 * zs + zi)

    peers = [(min(abs(k[0]), chips - abs(k[0])), member(k), fq) for k in order]
    peers += [(min(k, zs - k), tm, xi * zs + lax.rem(zi + k, zs)) for k in range(1, zs)]
    peers += [(min(k // 2, xs - k // 2), *across_x(k)[1]) for k in range(1, 2 * xs)]
    for _, t, f in sorted(peers, key=lambda peer: -peer[0]):
        greet(t, f)
    has_next = fq < freqs - 1
    has_prev = fq > 0
    next_turns = has_next & (zi == zs - 1)
    prev_turns = has_prev & (zi == 0)
    low_halo = (yi == 0) & has_prev
    high_halo = (yi == chips - 1) & has_next

    @pl.when(next_turns)
    def _():
        greet(tm, next_fq)

    @pl.when(prev_turns)
    def _():
        greet(tm, prev_fq)

    loads[0].wait()
    for r in range(0, all_rows, 16):
        x_full[r:r + 16, :] = x_half[r:r + 16, :].astype(jnp.float32)
    low_lanes = lax.broadcasted_iota(jnp.int32, (1, LANES), 1) < LANES // 2
    nothing = jnp.zeros((1, LANES), jnp.float32)
    for o in range(chips):
        for p in range(2):
            first = 2 * o * rows + p
            for r in range(0, rows, 8):
                stage[2 * o + p, r:r + 8, :] = x_full[pl.ds(first + 2 * r, 8, stride=2), :]
            after = first + 2 * rows
            high = x_full[after:after + 1, :] if o < chips - 1 else nothing
            low = x_full[first - 2:first - 1, :] if o > 0 else nothing
            stage[2 * o + p, rows:rows + 1, :] = jnp.where(low_lanes, high, low)
    for p in range(2):
        edge[0, p] = x_full[all_rows - 2 + p:all_rows - 1 + p, :]
        edge[1, p] = x_full[p:p + 1, :]

    expected = (groups - 1) + (zs - 1) + (2 * xs - 1)
    pl.semaphore_wait(barrier, expected + next_turns.astype(jnp.int32) + prev_turns.astype(jnp.int32))

    def remote(src, dst, s_sem, r_sem, to):
        return pltpu.make_async_remote_copy(
            src_ref=src, dst_ref=dst, send_sem=s_sem, recv_sem=r_sem, device_id=to, device_id_type=MESH)

    def all_of(ref, count, sem):
        block = ref.at[pl.ds(0, count)]
        pltpu.make_async_copy(block, block, sem).wait()

    def out_copy(k):
        to = member(k)
        return remote(stage.at[to], recv.at[tm], send_sem.at[0], recv_sem.at[0], (to, fq))

    def edge_copy(side, to):
        return remote(edge.at[side], beside.at[side], edge_send.at[side], edge_recv.at[side], (tm, to))

    def halo_copy(side, p):
        owner = p if side == 0 else last - 1 + p
        to = jnp.where(tm == owner, owner + 1 - 2 * p, owner)
        return tm == owner, remote(
            beside.at[side, p], halo.at[tm], halo_send.at[side, p], halo_recv.at[0], (to, fq))

    def halo_pass(side):
        edge_copy(side, fq).wait_recv()
        for p in range(2):
            here, copy = halo_copy(side, p)

            @pl.when(here)
            def _():
                pltpu.make_async_copy(beside.at[side, p], halo.at[tm], halo_recv.at[0]).start()

            @pl.when(jnp.logical_not(here))
            def _():
                copy.start()

    def halo_sent(side):
        for p in range(2):
            here, copy = halo_copy(side, p)

            @pl.when(jnp.logical_not(here))
            def _():
                copy.wait_send()

    @pl.when(has_next)
    def _():
        edge_copy(0, next_fq).start()

    @pl.when(has_prev)
    def _():
        edge_copy(1, prev_fq).start()

    far = chips // 2
    near = far // 2
    direct = [k for k in order if k[0] != far]

    def relay_copy(src, dst, phase, c):
        way = near if c == 0 else -near
        return remote(src.at[member((far, lax.rem(core + c, 2)))], dst.at[c],
                      (send_sem, back_send)[phase].at[0], relay_recv.at[phase, c], (member((way, 0)), fq))

    def pass_copy(src, dst, r_sem, phase, c):
        way = near if c == 0 else -near
        origin = member((-way, 0))
        return remote(src.at[c], dst.at[origin], pass_send.at[phase], r_sem.at[0],
                      (member((way, lax.rem(core + c, 2))), fq))

    for c in (0, 1):
        relay_copy(stage, relay, 0, c).start()
    for k in direct:
        out_copy(k).start()

    @pl.when(has_prev)
    def _():
        halo_pass(0)

    @pl.when(has_next)
    def _():
        halo_pass(1)

    own = pltpu.make_async_copy(stage.at[tm], recv.at[tm], own_sem.at[0])
    own.start()

    for c in (0, 1):
        relay_copy(stage, relay, 0, c).wait_recv()
        pass_copy(relay, recv, recv_sem, 0, c).start()

    loads[1].wait()
    loads[2].wait()
    slot = lax.broadcasted_iota(jnp.int32, w_ref.shape, 1)
    weights = jnp.sum(jnp.where(slot == ids_ref[core], w_ref[...], 0.0), axis=1, keepdims=True)
    weights = weights / jnp.sum(weights, axis=0, keepdims=True)
    field = (rows + TAIL, LANES)
    staying, rising, falling = (jnp.broadcast_to(weights[i:i + 1, :], field) for i in range(3))
    lane = lax.broadcasted_iota(jnp.int32, field, 1)
    row_index = lax.broadcasted_iota(jnp.int32, field, 0)

    from_other = (high_halo & low_lanes) | (low_halo & jnp.logical_not(low_lanes))

    def emission_of(t):
        tail = jnp.where(from_other, halo[t], recv[t, rows:rows + 1, :])
        return jnp.concatenate([recv[t, 0:rows, :], jnp.broadcast_to(tail, (TAIL, LANES))], axis=0)

    def below(v):
        turned = pltpu.roll(v, 1, 1)
        return jnp.where(lane == 0, pltpu.roll(turned, 1, 0), turned)

    def above(v):
        turned = pltpu.roll(v, LANES - 1, 1)
        return jnp.where(lane == LANES - 1, pltpu.roll(turned, field[0] - 1, 0), turned)

    own.wait()
    all_of(recv, groups - 1, recv_sem.at[0])

    @pl.when(low_halo | high_halo)
    def _():
        all_of(halo, groups, halo_recv.at[0])

    world_low = (yi == 0) & (fq == 0)
    world_high = (yi == chips - 1) & (fq == freqs - 1)
    outside = ((row_index == rows) & world_high) | ((row_index > rows) & world_low)
    b = jnp.ones(field, jnp.float32)
    u = jnp.where(outside, 0.0, b)

    def forward(t, u):
        return emission_of(t) * (staying * u + rising * below(u) + falling * above(u))

    def backward(s, b):
        g = emission_of(s + 1) * b
        return staying * g + rising * above(g) + falling * below(g)

    half = groups // 2
    for step in range(half):
        u = forward(step, u)
        work[step] = u[:rows]
        if step > 0:
            b = backward(last - step, b)
        work[last - step] = b[:rows]
    b = backward(half - 1, b)
    middle = u[:rows] * b[:rows]
    work[half - 1] = middle
    part[...] = jnp.sum(middle, axis=0, keepdims=True)

    def spread(src, dst, to_of, mine, count, s_sem, r_sem):
        for k in range(1, count):
            remote(src, dst.at[mine], s_sem.at[0], r_sem.at[0], to_of(k)).start()

    def gather(src, dst, to_of, mine, count, s_sem, r_sem):
        all_of(dst, count - 1, r_sem.at[0])
        value = src[...]
        for k in range(1, count):
            value = value + dst[lax.rem(mine + k, count)]
        return value

    y_ring = (lambda k: (lax.rem(yi + k, chips) * 2 + core, fq), yi, chips, part_send, part_recv)
    z_ring = (lambda k: (tm, xi * zs + lax.rem(zi + k, zs)), zi, zs, z_send, z_recv)
    x_ring = (lambda k: across_x(k)[1], xi * 2 + core, 2 * xs, x_send, x_recv)
    spread(part, part_in, *y_ring)

    for step in range(half, groups):
        u = forward(step, u)
        work[step] = u[:rows] * work[step]
        if step > half:
            b = backward(last - step, b)
            work[last - step] = work[last - step] * b[:rows]

    def back_copy(k):
        to = member(k)
        return remote(work.at[to], home.at[tm], back_send.at[0], back_recv.at[0], (to, fq))

    own_back = pltpu.make_async_copy(work.at[tm], home.at[tm], own_sem.at[1])
    own_back.start()
    for c in (0, 1):
        relay_copy(work, relay_back, 1, c).start()
    for k in direct[:len(direct) // 2]:
        back_copy(k).start()

    z_part[...] = gather(part, part_in, *y_ring)
    spread(z_part, z_in, *z_ring)
    for k in direct[len(direct) // 2:]:
        back_copy(k).start()
    for c in (0, 1):
        relay_copy(work, relay_back, 1, c).wait_recv()
        pass_copy(relay_back, home, back_recv, 1, c).start()
    all_of(stage, groups - 1, send_sem.at[0])
    all_of(relay, 2, pass_send.at[0])

    x_part[...] = gather(z_part, z_in, *z_ring)
    spread(x_part, x_in, *x_ring)

    @pl.when(has_next)
    def _():
        edge_copy(0, next_fq).wait_send()
        halo_sent(1)

    @pl.when(has_prev)
    def _():
        edge_copy(1, prev_fq).wait_send()
        halo_sent(0)

    all_of(part_in, chips - 1, part_send.at[0])
    all_of(z_in, zs - 1, z_send.at[0])
    all_of(x_in, 2 * xs - 1, x_recv.at[0])
    same = x_part[...]
    other = jnp.zeros_like(same)
    for k in range(1, 2 * xs):
        place, _ = across_x(k)
        if k % 2 == 0:
            same = same + x_in[place]
        else:
            other = other + x_in[place]
    for p in range(2):
        whole = jnp.sum(jnp.where(core == p, same, other), axis=1, keepdims=True)
        total_ref[p:p + 1, :] = jnp.broadcast_to(whole, (1, LANES))

    own_back.wait()
    all_of(home, groups - 1, back_recv.at[0])
    all_of(x_in, 2 * xs - 1, x_send.at[0])
    all_of(work, groups - 1, back_send.at[0])
    all_of(relay_back, 2, pass_send.at[1])


def finish(bins, home, total_ref, out_hbm, level_hbm, out, level, sems):
    groups, rows = home.shape[0], home.shape[1]
    totals = [total_ref[p:p + 1, :] for p in range(2)]
    scales = [bins / total for total in totals]
    blocks = groups // 2
    copies = []
    for o in range(blocks):
        first = o * 2 * rows
        for p in range(2):
            for r in range(0, rows, 8):
                out[pl.ds(first + p + 2 * r, 8, stride=2), :] = home[2 * o + p, r:r + 8, :] * scales[p]
        block = pl.ds(first, 2 * rows)
        copies.append(pltpu.make_async_copy(out.at[block, :], out_hbm.at[block, :], sems.at[o]))
        copies[-1].start()
    for p in range(2):
        level[p] = (jnp.log(totals[p] * (1.0 / bins)) * (1.0 / groups))[0, 0]
    copies.append(pltpu.make_async_copy(level, level_hbm, sems.at[blocks]))
    copies[-1].start()
    for copy in copies:
        copy.wait()


def body(bins, groups, freqs, zs, emission, step_weights, template_ids):
    templates = emission.shape[1]
    here = emission.shape[2]
    total_rows = here // LANES
    all_rows = templates * total_rows
    rows = all_rows // groups
    xs = freqs // zs
    f32 = jnp.float32
    dma = pltpu.SemaphoreType.DMA
    lines = emission.reshape(templates, total_rows, LANES).transpose(1, 0, 2).reshape(all_rows, LANES)
    hbm = pl.BlockSpec(memory_space=pltpu.HBM)
    vmem = pl.BlockSpec(memory_space=pltpu.VMEM)
    home, total = pl.pallas_call(
        functools.partial(kernel, groups, freqs, zs, bins),
        out_shape=(
            jax.ShapeDtypeStruct((groups, rows, LANES), f32),
            jax.ShapeDtypeStruct((templates, LANES), f32),
        ),
        in_specs=[hbm, hbm, hbm],
        out_specs=(vmem, vmem),
        scratch_shapes=[
            pltpu.VMEM((all_rows, LANES), emission.dtype),
            pltpu.VMEM((all_rows, LANES), f32),
            pltpu.VMEM((step_weights.shape[1], step_weights.shape[0]), f32),
            pltpu.SMEM(template_ids.shape, jnp.int32),
            pltpu.VMEM((groups, rows + 1, LANES), f32),
            pltpu.VMEM((groups, rows + 1, LANES), f32),
            pltpu.VMEM((groups, 1, LANES), f32),
            pltpu.VMEM((2, 2, 1, LANES), f32),
            pltpu.VMEM((2, 2, 1, LANES), f32),
            pltpu.VMEM((groups, rows, LANES), f32),
            pltpu.VMEM((1, LANES), f32),
            pltpu.VMEM((groups // 2, 1, LANES), f32),
            pltpu.VMEM((1, LANES), f32),
            pltpu.VMEM((zs, 1, LANES), f32),
            pltpu.VMEM((1, LANES), f32),
            pltpu.VMEM((2 * xs, 1, LANES), f32),
            pltpu.VMEM((2, rows + 1, LANES), f32),
            pltpu.VMEM((2, rows, LANES), f32),
            dma((3,)), dma((1,)), dma((1,)), dma((2,)), dma((2,)), dma((2, 2)), dma((1,)), dma((1,)), dma((1,)),
            dma((1,)), dma((1,)), dma((1,)), dma((1,)), dma((1,)), dma((1,)), dma((2,)),
            dma((2, 2)), dma((2,)),
        ],
        compiler_params=pltpu.CompilerParams(
            collective_id=0, has_side_effects=True, vmem_limit_bytes=32 * 1024 * 1024
        ),
    )(*(pltpu.with_memory_space_constraint(v, pltpu.HBM) for v in (lines, step_weights.T, template_ids)))
    anywhere = pl.BlockSpec(memory_space=pl.ANY)
    post, level = pl.pallas_call(
        functools.partial(finish, bins),
        out_shape=(
            jax.ShapeDtypeStruct((all_rows, LANES), f32),
            jax.ShapeDtypeStruct((templates,), f32),
        ),
        in_specs=[vmem, vmem],
        out_specs=(anywhere, anywhere),
        scratch_shapes=[pltpu.VMEM((all_rows, LANES), f32), pltpu.SMEM((templates,), f32), dma((groups // 2 + 1,))],
        compiler_params=pltpu.CompilerParams(vmem_limit_bytes=4 * 1024 * 1024),
    )(home, total)
    posterior = post.reshape(total_rows, templates, LANES).transpose(1, 0, 2).reshape(1, templates, here)
    return posterior, level


def solution(mesh):
    groups, freqs = mesh.shape["tm"], mesh.shape["freq"]
    zs = min(Z_CHIPS, freqs // 2)

    def whole(emission, step_weights, template_ids):
        return jax.shard_map(
            functools.partial(body, emission.shape[2], groups, freqs, zs),
            mesh=mesh,
            in_specs=(P("tm", None, "freq"), P(), P()),
            out_specs=(P("tm", None, "freq"), P()),
            check_vma=False,
        )(emission, step_weights, template_ids)

    return whole
```

```python
import functools

import jax
import jax.numpy as jnp
from jax import lax
from jax.experimental import pallas as pl
from jax.experimental.pallas import tpu as pltpu
from jax.sharding import PartitionSpec as P

MESH = pl.DeviceIdType.MESH
Z_CHIPS = 8
LANES = 128
TAIL = 8


def ring_order(chips):
    steps = [chips // 2]
    for d in range(chips // 2 - 1, 0, -1):
        steps += [-d, d]
    return [(d, c) for d in steps for c in (0, 1)] + [(0, 1)]


def kernel(groups, freqs, zs, bins, x_hbm, w_hbm, ids_hbm, home, total_ref,
           x_half, x_full, w_ref, ids_ref, stage, recv, halo, edge, beside, work,
           part, part_in, z_part, z_in, x_part, x_in, relay, relay_back,
           load_sem, send_sem, recv_sem, edge_send, edge_recv, halo_send, halo_recv, back_send, back_recv,
           part_send, part_recv, z_send, z_recv, x_send, x_recv, own_sem,
           relay_recv, pass_send):
    xs = freqs // zs
    chips = groups // 2
    tm = lax.axis_index("tm")
    fq = lax.axis_index("freq")
    yi = tm // 2
    core = lax.rem(tm, 2)
    xi = fq // zs
    zi = lax.rem(fq, zs)
    next_fq = lax.rem(fq + 1, freqs)
    prev_fq = lax.rem(fq + freqs - 1, freqs)
    all_rows = x_hbm.shape[0]
    rows = all_rows // groups
    last = groups - 1
    order = ring_order(chips)

    def member(k):
        return lax.rem(yi + k[0] + chips, chips) * 2 + lax.rem(core + k[1], 2)

    loads = [pltpu.make_async_copy(src, dst, load_sem.at[i])
             for i, (src, dst) in enumerate(((x_hbm, x_half), (w_hbm, w_ref), (ids_hbm, ids_ref)))]
    for copy in loads:
        copy.start()

    barrier = pltpu.get_barrier_semaphore()

    def greet(t, f):
        pl.semaphore_signal(barrier, inc=1, device_id=(t, f), device_id_type=MESH)

    def across_x(k):
        place = lax.rem(xi * 2 + core + k, 2 * xs)
        return place, (yi * 2 + lax.rem(place, 2), place // 2 * zs + zi)

    peers = [(min(abs(k[0]), chips - abs(k[0])), member(k), fq) for k in order]
    peers += [(min(k, zs - k), tm, xi * zs + lax.rem(zi + k, zs)) for k in range(1, zs)]
    peers += [(min(k // 2, xs - k // 2), *across_x(k)[1]) for k in range(1, 2 * xs)]
    for _, t, f in sorted(peers, key=lambda peer: -peer[0]):
        greet(t, f)
    has_next = fq < freqs - 1
    has_prev = fq > 0
    next_turns = has_next & (zi == zs - 1)
    prev_turns = has_prev & (zi == 0)
    low_halo = (yi == 0) & has_prev
    high_halo = (yi == chips - 1) & has_next

    @pl.when(next_turns)
    def _():
        greet(tm, next_fq)

    @pl.when(prev_turns)
    def _():
        greet(tm, prev_fq)

    loads[0].wait()
    for r in range(0, all_rows, 16):
        x_full[r:r + 16, :] = x_half[r:r + 16, :].astype(jnp.float32)
    low_lanes = lax.broadcasted_iota(jnp.int32, (1, LANES), 1) < LANES // 2
    nothing = jnp.zeros((1, LANES), jnp.float32)
    for o in range(chips):
        for p in range(2):
            first = 2 * o * rows + p
            for r in range(0, rows, 8):
                stage[2 * o + p, r:r + 8, :] = x_full[pl.ds(first + 2 * r, 8, stride=2), :]
            after = first + 2 * rows
            high = x_full[after:after + 1, :] if o < chips - 1 else nothing
            low = x_full[first - 2:first - 1, :] if o > 0 else nothing
            stage[2 * o + p, rows:rows + 1, :] = jnp.where(low_lanes, high, low)
    for p in range(2):
        edge[0, p] = x_full[all_rows - 2 + p:all_rows - 1 + p, :]
        edge[1, p] = x_full[p:p + 1, :]

    expected = (groups - 1) + (zs - 1) + (2 * xs - 1)
    pl.semaphore_wait(barrier, expected + next_turns.astype(jnp.int32) + prev_turns.astype(jnp.int32))

    def remote(src, dst, s_sem, r_sem, to):
        return pltpu.make_async_remote_copy(
            src_ref=src, dst_ref=dst, send_sem=s_sem, recv_sem=r_sem, device_id=to, device_id_type=MESH)

    def all_of(ref, count, sem):
        block = ref.at[pl.ds(0, count)]
        pltpu.make_async_copy(block, block, sem).wait()

    def out_copy(k):
        to = member(k)
        return remote(stage.at[to], recv.at[tm], send_sem.at[0], recv_sem.at[0], (to, fq))

    def edge_copy(side, to):
        return remote(edge.at[side], beside.at[side], edge_send.at[side], edge_recv.at[side], (tm, to))

    def halo_copy(side, p):
        owner = p if side == 0 else last - 1 + p
        to = jnp.where(tm == owner, owner + 1 - 2 * p, owner)
        return tm == owner, remote(
            beside.at[side, p], halo.at[tm], halo_send.at[side, p], halo_recv.at[0], (to, fq))

    def halo_pass(side):
        edge_copy(side, fq).wait_recv()
        for p in range(2):
            here, copy = halo_copy(side, p)

            @pl.when(here)
            def _():
                pltpu.make_async_copy(beside.at[side, p], halo.at[tm], halo_recv.at[0]).start()

            @pl.when(jnp.logical_not(here))
            def _():
                copy.start()

    def halo_sent(side):
        for p in range(2):
            here, copy = halo_copy(side, p)

            @pl.when(jnp.logical_not(here))
            def _():
                copy.wait_send()

    @pl.when(has_next)
    def _():
        edge_copy(0, next_fq).start()

    @pl.when(has_prev)
    def _():
        edge_copy(1, prev_fq).start()

    far = chips // 2
    near = far // 2
    direct = [k for k in order if k[0] != far]

    def relay_copy(src, dst, phase, c):
        way = near if c == 0 else -near
        return remote(src.at[member((far, lax.rem(core + c, 2)))], dst.at[c],
                      (send_sem, back_send)[phase].at[0], relay_recv.at[phase, c], (member((way, 0)), fq))

    def pass_copy(src, dst, r_sem, phase, c):
        way = near if c == 0 else -near
        origin = member((-way, 0))
        return remote(src.at[c], dst.at[origin], pass_send.at[phase], r_sem.at[0],
                      (member((way, lax.rem(core + c, 2))), fq))

    for c in (0, 1):
        relay_copy(stage, relay, 0, c).start()
    for k in direct:
        out_copy(k).start()

    @pl.when(has_prev)
    def _():
        halo_pass(0)

    @pl.when(has_next)
    def _():
        halo_pass(1)

    own = pltpu.make_async_copy(stage.at[tm], recv.at[tm], own_sem.at[0])
    own.start()

    for c in (0, 1):
        relay_copy(stage, relay, 0, c).wait_recv()
        pass_copy(relay, recv, recv_sem, 0, c).start()

    loads[1].wait()
    loads[2].wait()
    slot = lax.broadcasted_iota(jnp.int32, w_ref.shape, 1)
    weights = jnp.sum(jnp.where(slot == ids_ref[core], w_ref[...], 0.0), axis=1, keepdims=True)
    weights = weights / jnp.sum(weights, axis=0, keepdims=True)
    field = (rows + TAIL, LANES)
    staying, rising, falling = (jnp.broadcast_to(weights[i:i + 1, :], field) for i in range(3))
    lane = lax.broadcasted_iota(jnp.int32, field, 1)
    row_index = lax.broadcasted_iota(jnp.int32, field, 0)

    from_other = (high_halo & low_lanes) | (low_halo & jnp.logical_not(low_lanes))

    def emission_of(t):
        tail = jnp.where(from_other, halo[t], recv[t, rows:rows + 1, :])
        return jnp.concatenate([recv[t, 0:rows, :], jnp.broadcast_to(tail, (TAIL, LANES))], axis=0)

    def below(v, by=1):
        turned = pltpu.roll(v, by, 1)
        return jnp.where(lane < by, pltpu.roll(turned, 1, 0), turned)

    def above(v, by=1):
        turned = pltpu.roll(v, LANES - by, 1)
        return jnp.where(lane >= LANES - by, pltpu.roll(turned, field[0] - 1, 0), turned)

    own.wait()
    all_of(recv, groups - 1, recv_sem.at[0])

    @pl.when(low_halo | high_halo)
    def _():
        all_of(halo, groups, halo_recv.at[0])

    world_low = (yi == 0) & (fq == 0)
    world_high = (yi == chips - 1) & (fq == freqs - 1)
    outside = ((row_index == rows) & world_high) | ((row_index > rows) & world_low)
    b = jnp.ones(field, jnp.float32)
    u = jnp.where(outside, 0.0, b)

    def forward_two(t, u):
        e = emission_of(t)
        low, low2, high, high2 = below(u), below(u, 2), above(u), above(u, 2)
        first = e * (staying * u + rising * low + falling * high)
        first_low = below(e) * (staying * low + rising * low2 + falling * u)
        first_high = above(e) * (staying * high + rising * u + falling * high2)
        return first, emission_of(t + 1) * (staying * first + rising * first_low + falling * first_high)

    def backward_two(s, b):
        g = emission_of(s + 1) * b
        low, low2, high, high2 = below(g), below(g, 2), above(g), above(g, 2)
        first = staying * g + rising * high + falling * low
        if s == 0:
            return first, None
        e = emission_of(s)
        first_low = below(e) * (staying * low + rising * g + falling * low2)
        first_high = above(e) * (staying * high + rising * high2 + falling * g)
        return first, staying * (e * first) + rising * first_high + falling * first_low

    half = groups // 2
    work[last] = b[:rows]
    for step in range(0, half, 2):
        first, u = forward_two(step, u)
        work[step] = first[:rows]
        if step + 1 < half - 1:
            work[step + 1] = u[:rows]
        first, b = backward_two(last - 1 - step, b)
        work[last - 1 - step] = first[:rows]
        if step + 1 < half - 1:
            work[last - 2 - step] = b[:rows]
    middle = u[:rows] * b[:rows]
    work[half - 1] = middle
    part[...] = jnp.sum(middle, axis=0, keepdims=True)

    def spread(src, dst, to_of, mine, count, s_sem, r_sem):
        for k in range(1, count):
            remote(src, dst.at[mine], s_sem.at[0], r_sem.at[0], to_of(k)).start()

    def gather(src, dst, to_of, mine, count, s_sem, r_sem):
        all_of(dst, count - 1, r_sem.at[0])
        value = src[...]
        for k in range(1, count):
            value = value + dst[lax.rem(mine + k, count)]
        return value

    y_ring = (lambda k: (lax.rem(yi + k, chips) * 2 + core, fq), yi, chips, part_send, part_recv)
    z_ring = (lambda k: (tm, xi * zs + lax.rem(zi + k, zs)), zi, zs, z_send, z_recv)
    x_ring = (lambda k: across_x(k)[1], xi * 2 + core, 2 * xs, x_send, x_recv)
    spread(part, part_in, *y_ring)

    for step in range(half, groups, 2):
        first, u = forward_two(step, u)
        work[step] = first[:rows] * work[step]
        work[step + 1] = u[:rows] * work[step + 1]
        first, b = backward_two(last - 1 - step, b)
        work[last - 1 - step] = work[last - 1 - step] * first[:rows]
        if b is not None:
            work[last - 2 - step] = work[last - 2 - step] * b[:rows]

    def back_copy(k):
        to = member(k)
        return remote(work.at[to], home.at[tm], back_send.at[0], back_recv.at[0], (to, fq))

    own_back = pltpu.make_async_copy(work.at[tm], home.at[tm], own_sem.at[1])
    own_back.start()
    for c in (0, 1):
        relay_copy(work, relay_back, 1, c).start()
    for k in direct[:len(direct) // 2]:
        back_copy(k).start()

    z_part[...] = gather(part, part_in, *y_ring)
    spread(z_part, z_in, *z_ring)
    for k in direct[len(direct) // 2:]:
        back_copy(k).start()
    for c in (0, 1):
        relay_copy(work, relay_back, 1, c).wait_recv()
        pass_copy(relay_back, home, back_recv, 1, c).start()
    all_of(stage, groups - 1, send_sem.at[0])
    all_of(relay, 2, pass_send.at[0])

    x_part[...] = gather(z_part, z_in, *z_ring)
    spread(x_part, x_in, *x_ring)

    @pl.when(has_next)
    def _():
        edge_copy(0, next_fq).wait_send()
        halo_sent(1)

    @pl.when(has_prev)
    def _():
        edge_copy(1, prev_fq).wait_send()
        halo_sent(0)

    all_of(part_in, chips - 1, part_send.at[0])
    all_of(z_in, zs - 1, z_send.at[0])
    all_of(x_in, 2 * xs - 1, x_recv.at[0])
    same = x_part[...]
    other = jnp.zeros_like(same)
    for k in range(1, 2 * xs):
        place, _ = across_x(k)
        if k % 2 == 0:
            same = same + x_in[place]
        else:
            other = other + x_in[place]
    for p in range(2):
        whole = jnp.sum(jnp.where(core == p, same, other), axis=1, keepdims=True)
        total_ref[p:p + 1, :] = jnp.broadcast_to(whole, (1, LANES))

    own_back.wait()
    all_of(home, groups - 1, back_recv.at[0])
    all_of(x_in, 2 * xs - 1, x_send.at[0])
    all_of(work, groups - 1, back_send.at[0])
    all_of(relay_back, 2, pass_send.at[1])


def finish(bins, home, total_ref, out_hbm, level_hbm, out, level, sems):
    groups, rows = home.shape[0], home.shape[1]
    totals = [total_ref[p:p + 1, :] for p in range(2)]
    scales = [bins / total for total in totals]
    blocks = groups // 2
    copies = []
    for o in range(blocks):
        first = o * 2 * rows
        for p in range(2):
            for r in range(0, rows, 8):
                out[pl.ds(first + p + 2 * r, 8, stride=2), :] = home[2 * o + p, r:r + 8, :] * scales[p]
        block = pl.ds(first, 2 * rows)
        copies.append(pltpu.make_async_copy(out.at[block, :], out_hbm.at[block, :], sems.at[o]))
        copies[-1].start()
    for p in range(2):
        level[p] = (jnp.log(totals[p] * (1.0 / bins)) * (1.0 / groups))[0, 0]
    copies.append(pltpu.make_async_copy(level, level_hbm, sems.at[blocks]))
    copies[-1].start()
    for copy in copies:
        copy.wait()


def body(bins, groups, freqs, zs, emission, step_weights, template_ids):
    templates = emission.shape[1]
    here = emission.shape[2]
    total_rows = here // LANES
    all_rows = templates * total_rows
    rows = all_rows // groups
    xs = freqs // zs
    f32 = jnp.float32
    dma = pltpu.SemaphoreType.DMA
    lines = emission.reshape(templates, total_rows, LANES).transpose(1, 0, 2).reshape(all_rows, LANES)
    hbm = pl.BlockSpec(memory_space=pltpu.HBM)
    vmem = pl.BlockSpec(memory_space=pltpu.VMEM)
    home, total = pl.pallas_call(
        functools.partial(kernel, groups, freqs, zs, bins),
        out_shape=(
            jax.ShapeDtypeStruct((groups, rows, LANES), f32),
            jax.ShapeDtypeStruct((templates, LANES), f32),
        ),
        in_specs=[hbm, hbm, hbm],
        out_specs=(vmem, vmem),
        scratch_shapes=[
            pltpu.VMEM((all_rows, LANES), emission.dtype),
            pltpu.VMEM((all_rows, LANES), f32),
            pltpu.VMEM((step_weights.shape[1], step_weights.shape[0]), f32),
            pltpu.SMEM(template_ids.shape, jnp.int32),
            pltpu.VMEM((groups, rows + 1, LANES), f32),
            pltpu.VMEM((groups, rows + 1, LANES), f32),
            pltpu.VMEM((groups, 1, LANES), f32),
            pltpu.VMEM((2, 2, 1, LANES), f32),
            pltpu.VMEM((2, 2, 1, LANES), f32),
            pltpu.VMEM((groups, rows, LANES), f32),
            pltpu.VMEM((1, LANES), f32),
            pltpu.VMEM((groups // 2, 1, LANES), f32),
            pltpu.VMEM((1, LANES), f32),
            pltpu.VMEM((zs, 1, LANES), f32),
            pltpu.VMEM((1, LANES), f32),
            pltpu.VMEM((2 * xs, 1, LANES), f32),
            pltpu.VMEM((2, rows + 1, LANES), f32),
            pltpu.VMEM((2, rows, LANES), f32),
            dma((3,)), dma((1,)), dma((1,)), dma((2,)), dma((2,)), dma((2, 2)), dma((1,)), dma((1,)), dma((1,)),
            dma((1,)), dma((1,)), dma((1,)), dma((1,)), dma((1,)), dma((1,)), dma((2,)),
            dma((2, 2)), dma((2,)),
        ],
        compiler_params=pltpu.CompilerParams(
            collective_id=0, has_side_effects=True, vmem_limit_bytes=32 * 1024 * 1024
        ),
    )(*(pltpu.with_memory_space_constraint(v, pltpu.HBM) for v in (lines, step_weights.T, template_ids)))
    anywhere = pl.BlockSpec(memory_space=pl.ANY)
    post, level = pl.pallas_call(
        functools.partial(finish, bins),
        out_shape=(
            jax.ShapeDtypeStruct((all_rows, LANES), f32),
            jax.ShapeDtypeStruct((templates,), f32),
        ),
        in_specs=[vmem, vmem],
        out_specs=(anywhere, anywhere),
        scratch_shapes=[pltpu.VMEM((all_rows, LANES), f32), pltpu.SMEM((templates,), f32), dma((groups // 2 + 1,))],
        compiler_params=pltpu.CompilerParams(vmem_limit_bytes=4 * 1024 * 1024),
    )(home, total)
    posterior = post.reshape(total_rows, templates, LANES).transpose(1, 0, 2).reshape(1, templates, here)
    return posterior, level


def solution(mesh):
    groups, freqs = mesh.shape["tm"], mesh.shape["freq"]
    zs = min(Z_CHIPS, freqs // 2)

    def whole(emission, step_weights, template_ids):
        return jax.shard_map(
            functools.partial(body, emission.shape[2], groups, freqs, zs),
            mesh=mesh,
            in_specs=(P("tm", None, "freq"), P(), P()),
            out_specs=(P("tm", None, "freq"), P()),
            check_vma=False,
        )(emission, step_weights, template_ids)

    return whole
```

```python
import functools

import jax
import jax.numpy as jnp
from jax import lax
from jax.experimental import pallas as pl
from jax.experimental.pallas import tpu as pltpu
from jax.sharding import PartitionSpec as P

MESH = pl.DeviceIdType.MESH
Z_CHIPS = 8
LANES = 128
TAIL = 8


def ring_order(chips):
    steps = [chips // 2]
    for d in range(chips // 2 - 1, 0, -1):
        steps += [-d, d]
    return [(d, c) for d in steps for c in (0, 1)] + [(0, 1)]


def kernel(groups, freqs, zs, bins, x_hbm, w_hbm, ids_hbm, home, total_ref,
           x_half, x_full, w_ref, ids_ref, stage, recv, halo, edge, beside, work,
           part, part_in, z_part, z_in, x_part, x_in, relay, relay_back,
           load_sem, send_sem, recv_sem, edge_send, edge_recv, halo_send, halo_recv, back_send, back_recv,
           part_send, part_recv, z_send, z_recv, x_send, x_recv, own_sem,
           relay_recv, pass_send):
    xs = freqs // zs
    chips = groups // 2
    tm = lax.axis_index("tm")
    fq = lax.axis_index("freq")
    yi = tm // 2
    core = lax.rem(tm, 2)
    xi = fq // zs
    zi = lax.rem(fq, zs)
    next_fq = lax.rem(fq + 1, freqs)
    prev_fq = lax.rem(fq + freqs - 1, freqs)
    all_rows = x_hbm.shape[0]
    rows = all_rows // groups
    last = groups - 1
    order = ring_order(chips)

    def member(k):
        return lax.rem(yi + k[0] + chips, chips) * 2 + lax.rem(core + k[1], 2)

    loads = [pltpu.make_async_copy(src, dst, load_sem.at[i])
             for i, (src, dst) in enumerate(((x_hbm, x_half), (w_hbm, w_ref), (ids_hbm, ids_ref)))]
    for copy in loads:
        copy.start()

    barrier = pltpu.get_barrier_semaphore()

    def greet(t, f):
        pl.semaphore_signal(barrier, inc=1, device_id=(t, f), device_id_type=MESH)

    def across_x(k):
        place = lax.rem(xi * 2 + core + k, 2 * xs)
        return place, (yi * 2 + lax.rem(place, 2), place // 2 * zs + zi)

    peers = [(min(abs(k[0]), chips - abs(k[0])), member(k), fq) for k in order]
    peers += [(min(k, zs - k), tm, xi * zs + lax.rem(zi + k, zs)) for k in range(1, zs)]
    peers += [(min(k // 2, xs - k // 2), *across_x(k)[1]) for k in range(1, 2 * xs)]
    for _, t, f in sorted(peers, key=lambda peer: -peer[0]):
        greet(t, f)
    has_next = fq < freqs - 1
    has_prev = fq > 0
    next_turns = has_next & (zi == zs - 1)
    prev_turns = has_prev & (zi == 0)
    low_halo = (yi == 0) & has_prev
    high_halo = (yi == chips - 1) & has_next

    @pl.when(next_turns)
    def _():
        greet(tm, next_fq)

    @pl.when(prev_turns)
    def _():
        greet(tm, prev_fq)

    loads[0].wait()
    for r in range(0, all_rows, 16):
        x_full[r:r + 16, :] = x_half[r:r + 16, :].astype(jnp.float32)
    low_lanes = lax.broadcasted_iota(jnp.int32, (1, LANES), 1) < LANES // 2
    nothing = jnp.zeros((1, LANES), jnp.float32)
    for o in range(chips):
        for p in range(2):
            first = 2 * o * rows + p
            for r in range(0, rows, 8):
                stage[2 * o + p, r:r + 8, :] = x_full[pl.ds(first + 2 * r, 8, stride=2), :]
            after = first + 2 * rows
            high = x_full[after:after + 1, :] if o < chips - 1 else nothing
            low = x_full[first - 2:first - 1, :] if o > 0 else nothing
            stage[2 * o + p, rows:rows + 1, :] = jnp.where(low_lanes, high, low)
    for p in range(2):
        edge[0, p] = x_full[all_rows - 2 + p:all_rows - 1 + p, :]
        edge[1, p] = x_full[p:p + 1, :]

    expected = (groups - 1) + (zs - 1) + (2 * xs - 1)
    pl.semaphore_wait(barrier, expected + next_turns.astype(jnp.int32) + prev_turns.astype(jnp.int32))

    def remote(src, dst, s_sem, r_sem, to):
        return pltpu.make_async_remote_copy(
            src_ref=src, dst_ref=dst, send_sem=s_sem, recv_sem=r_sem, device_id=to, device_id_type=MESH)

    def all_of(ref, count, sem):
        block = ref.at[pl.ds(0, count)]
        pltpu.make_async_copy(block, block, sem).wait()

    def out_copy(k):
        to = member(k)
        return remote(stage.at[to], recv.at[tm], send_sem.at[0], recv_sem.at[0], (to, fq))

    def edge_copy(side, to):
        return remote(edge.at[side], beside.at[side], edge_send.at[side], edge_recv.at[side], (tm, to))

    def halo_copy(side, p):
        owner = p if side == 0 else last - 1 + p
        to = jnp.where(tm == owner, owner + 1 - 2 * p, owner)
        return tm == owner, remote(
            beside.at[side, p], halo.at[tm], halo_send.at[side, p], halo_recv.at[0], (to, fq))

    def halo_pass(side):
        edge_copy(side, fq).wait_recv()
        for p in range(2):
            here, copy = halo_copy(side, p)

            @pl.when(here)
            def _():
                pltpu.make_async_copy(beside.at[side, p], halo.at[tm], halo_recv.at[0]).start()

            @pl.when(jnp.logical_not(here))
            def _():
                copy.start()

    def halo_sent(side):
        for p in range(2):
            here, copy = halo_copy(side, p)

            @pl.when(jnp.logical_not(here))
            def _():
                copy.wait_send()

    @pl.when(has_next)
    def _():
        edge_copy(0, next_fq).start()

    @pl.when(has_prev)
    def _():
        edge_copy(1, prev_fq).start()

    far = chips // 2
    near = far // 2
    direct = [k for k in order if k[0] != far]

    def relay_copy(src, dst, phase, c):
        way = near if c == 0 else -near
        return remote(src.at[member((far, lax.rem(core + c, 2)))], dst.at[c],
                      (send_sem, back_send)[phase].at[0], relay_recv.at[phase, c], (member((way, 0)), fq))

    def pass_copy(src, dst, r_sem, phase, c):
        way = near if c == 0 else -near
        origin = member((-way, 0))
        return remote(src.at[c], dst.at[origin], pass_send.at[phase], r_sem.at[0],
                      (member((way, lax.rem(core + c, 2))), fq))

    for c in (0, 1):
        relay_copy(stage, relay, 0, c).start()
    for k in direct[:len(direct) // 2]:
        out_copy(k).start()

    own = pltpu.make_async_copy(stage.at[tm], recv.at[tm], own_sem.at[0])
    own.start()

    @pl.when(has_prev)
    def _():
        halo_pass(0)

    @pl.when(has_next)
    def _():
        halo_pass(1)

    for c in (0, 1):
        relay_copy(stage, relay, 0, c).wait_recv()
        pass_copy(relay, recv, recv_sem, 0, c).start()
    for k in direct[len(direct) // 2:]:
        out_copy(k).start()

    loads[1].wait()
    loads[2].wait()
    slot = lax.broadcasted_iota(jnp.int32, w_ref.shape, 1)
    weights = jnp.sum(jnp.where(slot == ids_ref[core], w_ref[...], 0.0), axis=1, keepdims=True)
    weights = weights / jnp.sum(weights, axis=0, keepdims=True)
    field = (rows + TAIL, LANES)
    staying, rising, falling = (jnp.broadcast_to(weights[i:i + 1, :], field) for i in range(3))
    lane = lax.broadcasted_iota(jnp.int32, field, 1)
    row_index = lax.broadcasted_iota(jnp.int32, field, 0)

    from_other = (high_halo & low_lanes) | (low_halo & jnp.logical_not(low_lanes))

    def emission_of(t):
        tail = jnp.where(from_other, halo[t], recv[t, rows:rows + 1, :])
        return jnp.concatenate([recv[t, 0:rows, :], jnp.broadcast_to(tail, (TAIL, LANES))], axis=0)

    def below(v):
        turned = pltpu.roll(v, 1, 1)
        return jnp.where(lane == 0, pltpu.roll(turned, 1, 0), turned)

    def above(v):
        turned = pltpu.roll(v, LANES - 1, 1)
        return jnp.where(lane == LANES - 1, pltpu.roll(turned, field[0] - 1, 0), turned)

    own.wait()
    all_of(recv, groups - 1, recv_sem.at[0])

    @pl.when(low_halo | high_halo)
    def _():
        all_of(halo, groups, halo_recv.at[0])

    world_low = (yi == 0) & (fq == 0)
    world_high = (yi == chips - 1) & (fq == freqs - 1)
    outside = ((row_index == rows) & world_high) | ((row_index > rows) & world_low)
    b = jnp.ones(field, jnp.float32)
    u = jnp.where(outside, 0.0, b)

    def forward(t, u):
        return emission_of(t) * (staying * u + rising * below(u) + falling * above(u))

    def backward(s, b):
        g = emission_of(s + 1) * b
        return staying * g + rising * above(g) + falling * below(g)

    half = groups // 2
    for step in range(half):
        u = forward(step, u)
        work[step] = u[:rows]
        if step > 0:
            b = backward(last - step, b)
        work[last - step] = b[:rows]
    b = backward(half - 1, b)
    middle = u[:rows] * b[:rows]
    work[half - 1] = middle
    part[...] = jnp.sum(middle, axis=0, keepdims=True)

    def spread(src, dst, to_of, mine, count, s_sem, r_sem):
        for k in range(1, count):
            remote(src, dst.at[mine], s_sem.at[0], r_sem.at[0], to_of(k)).start()

    def gather(src, dst, to_of, mine, count, s_sem, r_sem):
        all_of(dst, count - 1, r_sem.at[0])
        value = src[...]
        for k in range(1, count):
            value = value + dst[lax.rem(mine + k, count)]
        return value

    y_ring = (lambda k: (lax.rem(yi + k, chips) * 2 + core, fq), yi, chips, part_send, part_recv)
    z_ring = (lambda k: (tm, xi * zs + lax.rem(zi + k, zs)), zi, zs, z_send, z_recv)
    x_ring = (lambda k: across_x(k)[1], xi * 2 + core, 2 * xs, x_send, x_recv)
    spread(part, part_in, *y_ring)

    for step in range(half, groups):
        u = forward(step, u)
        work[step] = u[:rows] * work[step]
        if step > half:
            b = backward(last - step, b)
            work[last - step] = work[last - step] * b[:rows]

    def back_copy(k):
        to = member(k)
        return remote(work.at[to], home.at[tm], back_send.at[0], back_recv.at[0], (to, fq))

    own_back = pltpu.make_async_copy(work.at[tm], home.at[tm], own_sem.at[1])
    own_back.start()
    for c in (0, 1):
        relay_copy(work, relay_back, 1, c).start()
    for k in direct[:len(direct) // 2]:
        back_copy(k).start()

    z_part[...] = gather(part, part_in, *y_ring)
    spread(z_part, z_in, *z_ring)
    for c in (0, 1):
        relay_copy(work, relay_back, 1, c).wait_recv()
        pass_copy(relay_back, home, back_recv, 1, c).start()
    for k in direct[len(direct) // 2:]:
        back_copy(k).start()
    all_of(stage, groups - 1, send_sem.at[0])
    all_of(relay, 2, pass_send.at[0])

    x_part[...] = gather(z_part, z_in, *z_ring)
    spread(x_part, x_in, *x_ring)

    @pl.when(has_next)
    def _():
        edge_copy(0, next_fq).wait_send()
        halo_sent(1)

    @pl.when(has_prev)
    def _():
        edge_copy(1, prev_fq).wait_send()
        halo_sent(0)

    all_of(part_in, chips - 1, part_send.at[0])
    all_of(z_in, zs - 1, z_send.at[0])
    all_of(x_in, 2 * xs - 1, x_recv.at[0])
    same = x_part[...]
    other = jnp.zeros_like(same)
    for k in range(1, 2 * xs):
        place, _ = across_x(k)
        if k % 2 == 0:
            same = same + x_in[place]
        else:
            other = other + x_in[place]
    for p in range(2):
        whole = jnp.sum(jnp.where(core == p, same, other), axis=1, keepdims=True)
        total_ref[p:p + 1, :] = jnp.broadcast_to(whole, (1, LANES))

    own_back.wait()
    all_of(home, groups - 1, back_recv.at[0])
    all_of(x_in, 2 * xs - 1, x_send.at[0])
    all_of(work, groups - 1, back_send.at[0])
    all_of(relay_back, 2, pass_send.at[1])


def finish(bins, home, total_ref, out_hbm, level_hbm, out, level, sems):
    groups, rows = home.shape[0], home.shape[1]
    totals = [total_ref[p:p + 1, :] for p in range(2)]
    scales = [bins / total for total in totals]
    blocks = groups // 2
    copies = []
    for o in range(blocks):
        first = o * 2 * rows
        for p in range(2):
            for r in range(0, rows, 8):
                out[pl.ds(first + p + 2 * r, 8, stride=2), :] = home[2 * o + p, r:r + 8, :] * scales[p]
        block = pl.ds(first, 2 * rows)
        copies.append(pltpu.make_async_copy(out.at[block, :], out_hbm.at[block, :], sems.at[o]))
        copies[-1].start()
    for p in range(2):
        level[p] = (jnp.log(totals[p] * (1.0 / bins)) * (1.0 / groups))[0, 0]
    copies.append(pltpu.make_async_copy(level, level_hbm, sems.at[blocks]))
    copies[-1].start()
    for copy in copies:
        copy.wait()


def body(bins, groups, freqs, zs, emission, step_weights, template_ids):
    templates = emission.shape[1]
    here = emission.shape[2]
    total_rows = here // LANES
    all_rows = templates * total_rows
    rows = all_rows // groups
    xs = freqs // zs
    f32 = jnp.float32
    dma = pltpu.SemaphoreType.DMA
    lines = emission.reshape(templates, total_rows, LANES).transpose(1, 0, 2).reshape(all_rows, LANES)
    hbm = pl.BlockSpec(memory_space=pltpu.HBM)
    vmem = pl.BlockSpec(memory_space=pltpu.VMEM)
    home, total = pl.pallas_call(
        functools.partial(kernel, groups, freqs, zs, bins),
        out_shape=(
            jax.ShapeDtypeStruct((groups, rows, LANES), f32),
            jax.ShapeDtypeStruct((templates, LANES), f32),
        ),
        in_specs=[hbm, hbm, hbm],
        out_specs=(vmem, vmem),
        scratch_shapes=[
            pltpu.VMEM((all_rows, LANES), emission.dtype),
            pltpu.VMEM((all_rows, LANES), f32),
            pltpu.VMEM((step_weights.shape[1], step_weights.shape[0]), f32),
            pltpu.SMEM(template_ids.shape, jnp.int32),
            pltpu.VMEM((groups, rows + 1, LANES), f32),
            pltpu.VMEM((groups, rows + 1, LANES), f32),
            pltpu.VMEM((groups, 1, LANES), f32),
            pltpu.VMEM((2, 2, 1, LANES), f32),
            pltpu.VMEM((2, 2, 1, LANES), f32),
            pltpu.VMEM((groups, rows, LANES), f32),
            pltpu.VMEM((1, LANES), f32),
            pltpu.VMEM((groups // 2, 1, LANES), f32),
            pltpu.VMEM((1, LANES), f32),
            pltpu.VMEM((zs, 1, LANES), f32),
            pltpu.VMEM((1, LANES), f32),
            pltpu.VMEM((2 * xs, 1, LANES), f32),
            pltpu.VMEM((2, rows + 1, LANES), f32),
            pltpu.VMEM((2, rows, LANES), f32),
            dma((3,)), dma((1,)), dma((1,)), dma((2,)), dma((2,)), dma((2, 2)), dma((1,)), dma((1,)), dma((1,)),
            dma((1,)), dma((1,)), dma((1,)), dma((1,)), dma((1,)), dma((1,)), dma((2,)),
            dma((2, 2)), dma((2,)),
        ],
        compiler_params=pltpu.CompilerParams(
            collective_id=0, has_side_effects=True, vmem_limit_bytes=32 * 1024 * 1024
        ),
    )(*(pltpu.with_memory_space_constraint(v, pltpu.HBM) for v in (lines, step_weights.T, template_ids)))
    anywhere = pl.BlockSpec(memory_space=pl.ANY)
    post, level = pl.pallas_call(
        functools.partial(finish, bins),
        out_shape=(
            jax.ShapeDtypeStruct((all_rows, LANES), f32),
            jax.ShapeDtypeStruct((templates,), f32),
        ),
        in_specs=[vmem, vmem],
        out_specs=(anywhere, anywhere),
        scratch_shapes=[pltpu.VMEM((all_rows, LANES), f32), pltpu.SMEM((templates,), f32), dma((groups // 2 + 1,))],
        compiler_params=pltpu.CompilerParams(vmem_limit_bytes=4 * 1024 * 1024),
    )(home, total)
    posterior = post.reshape(total_rows, templates, LANES).transpose(1, 0, 2).reshape(1, templates, here)
    return posterior, level


def solution(mesh):
    groups, freqs = mesh.shape["tm"], mesh.shape["freq"]
    zs = min(Z_CHIPS, freqs // 2)

    def whole(emission, step_weights, template_ids):
        return jax.shard_map(
            functools.partial(body, emission.shape[2], groups, freqs, zs),
            mesh=mesh,
            in_specs=(P("tm", None, "freq"), P(), P()),
            out_specs=(P("tm", None, "freq"), P()),
            check_vma=False,
        )(emission, step_weights, template_ids)

    return whole
```

```python
import functools

import jax
import jax.numpy as jnp
from jax import lax
from jax.experimental import pallas as pl
from jax.experimental.pallas import tpu as pltpu
from jax.sharding import PartitionSpec as P

MESH = pl.DeviceIdType.MESH
Z_CHIPS = 8
LANES = 128
TAIL = 8


def ring_order(chips):
    steps = [chips // 2]
    for d in range(chips // 2 - 1, 0, -1):
        steps += [-d, d]
    return [(d, c) for d in steps for c in (0, 1)] + [(0, 1)]


def kernel(groups, freqs, zs, bins, x_hbm, w_hbm, ids_hbm, home, total_ref,
           x_half, x_full, w_ref, ids_ref, stage, recv, halo, edge, beside, work,
           part, part_in, z_part, z_in, x_part, x_in,
           load_sem, send_sem, recv_sem, edge_send, edge_recv, halo_send, halo_recv, back_send, back_recv,
           part_send, part_recv, z_send, z_recv, x_send, x_recv, own_sem):
    xs = freqs // zs
    chips = groups // 2
    tm = lax.axis_index("tm")
    fq = lax.axis_index("freq")
    yi = tm // 2
    core = lax.rem(tm, 2)
    xi = fq // zs
    zi = lax.rem(fq, zs)
    next_fq = lax.rem(fq + 1, freqs)
    prev_fq = lax.rem(fq + freqs - 1, freqs)
    all_rows = x_hbm.shape[0]
    rows = all_rows // groups
    last = groups - 1
    order = ring_order(chips)

    def member(k):
        return lax.rem(yi + k[0] + chips, chips) * 2 + lax.rem(core + k[1], 2)

    loads = [pltpu.make_async_copy(src, dst, load_sem.at[i])
             for i, (src, dst) in enumerate(((x_hbm, x_half), (w_hbm, w_ref), (ids_hbm, ids_ref)))]
    for copy in loads:
        copy.start()

    barrier = pltpu.get_barrier_semaphore()

    def greet(t, f):
        pl.semaphore_signal(barrier, inc=1, device_id=(t, f), device_id_type=MESH)

    def across_x(k):
        place = lax.rem(xi * 2 + core + k, 2 * xs)
        return place, (yi * 2 + lax.rem(place, 2), place // 2 * zs + zi)

    peers = [(min(abs(k[0]), chips - abs(k[0])), member(k), fq) for k in order]
    peers += [(min(k, zs - k), tm, xi * zs + lax.rem(zi + k, zs)) for k in range(1, zs)]
    peers += [(min(k // 2, xs - k // 2), *across_x(k)[1]) for k in range(1, 2 * xs)]
    for _, t, f in sorted(peers, key=lambda peer: -peer[0]):
        greet(t, f)
    has_next = fq < freqs - 1
    has_prev = fq > 0
    next_turns = has_next & (zi == zs - 1)
    prev_turns = has_prev & (zi == 0)
    low_halo = (yi == 0) & has_prev
    high_halo = (yi == chips - 1) & has_next

    @pl.when(next_turns)
    def _():
        greet(tm, next_fq)

    @pl.when(prev_turns)
    def _():
        greet(tm, prev_fq)

    loads[0].wait()
    for r in range(0, all_rows, 16):
        x_full[r:r + 16, :] = x_half[r:r + 16, :].astype(jnp.float32)
    low_lanes = lax.broadcasted_iota(jnp.int32, (1, LANES), 1) < LANES // 2
    nothing = jnp.zeros((1, LANES), jnp.float32)
    for o in range(chips):
        for p in range(2):
            first = 2 * o * rows + p
            for r in range(0, rows, 8):
                stage[2 * o + p, r:r + 8, :] = x_full[pl.ds(first + 2 * r, 8, stride=2), :]
            after = first + 2 * rows
            high = x_full[after:after + 1, :] if o < chips - 1 else nothing
            low = x_full[first - 2:first - 1, :] if o > 0 else nothing
            stage[2 * o + p, rows:rows + 1, :] = jnp.where(low_lanes, high, low)
    for p in range(2):
        edge[0, p] = x_full[all_rows - 2 + p:all_rows - 1 + p, :]
        edge[1, p] = x_full[p:p + 1, :]

    expected = (groups - 1) + (zs - 1) + (2 * xs - 1)
    pl.semaphore_wait(barrier, expected + next_turns.astype(jnp.int32) + prev_turns.astype(jnp.int32))

    def remote(src, dst, s_sem, r_sem, to):
        return pltpu.make_async_remote_copy(
            src_ref=src, dst_ref=dst, send_sem=s_sem, recv_sem=r_sem, device_id=to, device_id_type=MESH)

    def all_of(ref, count, sem):
        block = ref.at[pl.ds(0, count)]
        pltpu.make_async_copy(block, block, sem).wait()

    def out_copy(k):
        to = member(k)
        return remote(stage.at[to], recv.at[tm], send_sem.at[0], recv_sem.at[0], (to, fq))

    def edge_copy(side, to):
        return remote(edge.at[side], beside.at[side], edge_send.at[side], edge_recv.at[side], (tm, to))

    def halo_copy(side, p):
        owner = p if side == 0 else last - 1 + p
        to = jnp.where(tm == owner, owner + 1 - 2 * p, owner)
        return tm == owner, remote(
            beside.at[side, p], halo.at[tm], halo_send.at[side, p], halo_recv.at[0], (to, fq))

    def halo_pass(side):
        edge_copy(side, fq).wait_recv()
        for p in range(2):
            here, copy = halo_copy(side, p)

            @pl.when(here)
            def _():
                pltpu.make_async_copy(beside.at[side, p], halo.at[tm], halo_recv.at[0]).start()

            @pl.when(jnp.logical_not(here))
            def _():
                copy.start()

    def halo_sent(side):
        for p in range(2):
            here, copy = halo_copy(side, p)

            @pl.when(jnp.logical_not(here))
            def _():
                copy.wait_send()

    @pl.when(has_next)
    def _():
        edge_copy(0, next_fq).start()

    @pl.when(has_prev)
    def _():
        edge_copy(1, prev_fq).start()

    for k in order:
        out_copy(k).start()

    @pl.when(has_prev)
    def _():
        halo_pass(0)

    @pl.when(has_next)
    def _():
        halo_pass(1)

    own = pltpu.make_async_copy(stage.at[tm], recv.at[tm], own_sem.at[0])
    own.start()

    loads[1].wait()
    loads[2].wait()
    slot = lax.broadcasted_iota(jnp.int32, w_ref.shape, 1)
    weights = jnp.sum(jnp.where(slot == ids_ref[core], w_ref[...], 0.0), axis=1, keepdims=True)
    weights = weights / jnp.sum(weights, axis=0, keepdims=True)
    field = (rows + TAIL, LANES)
    staying, rising, falling = (jnp.broadcast_to(weights[i:i + 1, :], field) for i in range(3))
    lane = lax.broadcasted_iota(jnp.int32, field, 1)
    row_index = lax.broadcasted_iota(jnp.int32, field, 0)

    from_other = (high_halo & low_lanes) | (low_halo & jnp.logical_not(low_lanes))

    def emission_of(t):
        tail = jnp.where(from_other, halo[t], recv[t, rows:rows + 1, :])
        return jnp.concatenate([recv[t, 0:rows, :], jnp.broadcast_to(tail, (TAIL, LANES))], axis=0)

    def below(v):
        turned = pltpu.roll(v, 1, 1)
        return jnp.where(lane == 0, pltpu.roll(turned, 1, 0), turned)

    def above(v):
        turned = pltpu.roll(v, LANES - 1, 1)
        return jnp.where(lane == LANES - 1, pltpu.roll(turned, field[0] - 1, 0), turned)

    own.wait()
    all_of(recv, groups - 1, recv_sem.at[0])

    @pl.when(low_halo | high_halo)
    def _():
        all_of(halo, groups, halo_recv.at[0])

    world_low = (yi == 0) & (fq == 0)
    world_high = (yi == chips - 1) & (fq == freqs - 1)
    outside = ((row_index == rows) & world_high) | ((row_index > rows) & world_low)
    b = jnp.ones(field, jnp.float32)
    u = jnp.where(outside, 0.0, b)

    def forward(t, u):
        return emission_of(t) * (staying * u + rising * below(u) + falling * above(u))

    def backward(s, b):
        g = emission_of(s + 1) * b
        return staying * g + rising * above(g) + falling * below(g)

    half = groups // 2
    for step in range(half):
        u = forward(step, u)
        work[step] = u[:rows]
        if step > 0:
            b = backward(last - step, b)
        work[last - step] = b[:rows]
    b = backward(half - 1, b)
    middle = u[:rows] * b[:rows]
    work[half - 1] = middle
    part[...] = jnp.sum(middle, axis=0, keepdims=True)

    def spread(src, dst, to_of, mine, count, s_sem, r_sem):
        for k in range(1, count):
            remote(src, dst.at[mine], s_sem.at[0], r_sem.at[0], to_of(k)).start()

    def gather(src, dst, to_of, mine, count, s_sem, r_sem):
        all_of(dst, count - 1, r_sem.at[0])
        value = src[...]
        for k in range(1, count):
            value = value + dst[lax.rem(mine + k, count)]
        return value

    y_ring = (lambda k: (lax.rem(yi + k, chips) * 2 + core, fq), yi, chips, part_send, part_recv)
    z_ring = (lambda k: (tm, xi * zs + lax.rem(zi + k, zs)), zi, zs, z_send, z_recv)
    x_ring = (lambda k: across_x(k)[1], xi * 2 + core, 2 * xs, x_send, x_recv)
    spread(part, part_in, *y_ring)

    for step in range(half, groups):
        u = forward(step, u)
        work[step] = u[:rows] * work[step]
        if step > half:
            b = backward(last - step, b)
            work[last - step] = work[last - step] * b[:rows]

    def back_copy(k):
        to = member(k)
        return remote(work.at[to], home.at[tm], back_send.at[0], back_recv.at[0], (to, fq))

    own_back = pltpu.make_async_copy(work.at[tm], home.at[tm], own_sem.at[1])
    own_back.start()
    for k in order[:len(order) // 2]:
        back_copy(k).start()

    z_part[...] = gather(part, part_in, *y_ring)
    spread(z_part, z_in, *z_ring)
    for k in order[len(order) // 2:]:
        back_copy(k).start()
    all_of(stage, groups - 1, send_sem.at[0])

    x_part[...] = gather(z_part, z_in, *z_ring)
    spread(x_part, x_in, *x_ring)

    @pl.when(has_next)
    def _():
        edge_copy(0, next_fq).wait_send()
        halo_sent(1)

    @pl.when(has_prev)
    def _():
        edge_copy(1, prev_fq).wait_send()
        halo_sent(0)

    all_of(part_in, chips - 1, part_send.at[0])
    all_of(z_in, zs - 1, z_send.at[0])
    all_of(x_in, 2 * xs - 1, x_recv.at[0])
    same = x_part[...]
    other = jnp.zeros_like(same)
    for k in range(1, 2 * xs):
        place, _ = across_x(k)
        if k % 2 == 0:
            same = same + x_in[place]
        else:
            other = other + x_in[place]
    for p in range(2):
        whole = jnp.sum(jnp.where(core == p, same, other), axis=1, keepdims=True)
        total_ref[p:p + 1, :] = jnp.broadcast_to(whole, (1, LANES))

    own_back.wait()
    all_of(home, groups - 1, back_recv.at[0])
    all_of(x_in, 2 * xs - 1, x_send.at[0])
    all_of(work, groups - 1, back_send.at[0])


def finish(bins, home, total_ref, out_hbm, level_hbm, out, level, sems):
    groups, rows = home.shape[0], home.shape[1]
    totals = [total_ref[p:p + 1, :] for p in range(2)]
    scales = [bins / total for total in totals]
    blocks = groups // 2
    copies = []
    for o in range(blocks):
        first = o * 2 * rows
        for p in range(2):
            for r in range(0, rows, 8):
                out[pl.ds(first + p + 2 * r, 8, stride=2), :] = home[2 * o + p, r:r + 8, :] * scales[p]
        block = pl.ds(first, 2 * rows)
        copies.append(pltpu.make_async_copy(out.at[block, :], out_hbm.at[block, :], sems.at[o]))
        copies[-1].start()
    for p in range(2):
        level[p] = (jnp.log(totals[p] * (1.0 / bins)) * (1.0 / groups))[0, 0]
    copies.append(pltpu.make_async_copy(level, level_hbm, sems.at[blocks]))
    copies[-1].start()
    for copy in copies:
        copy.wait()


def body(bins, groups, freqs, zs, emission, step_weights, template_ids):
    templates = emission.shape[1]
    here = emission.shape[2]
    total_rows = here // LANES
    all_rows = templates * total_rows
    rows = all_rows // groups
    xs = freqs // zs
    f32 = jnp.float32
    dma = pltpu.SemaphoreType.DMA
    lines = emission.reshape(templates, total_rows, LANES).transpose(1, 0, 2).reshape(all_rows, LANES)
    hbm = pl.BlockSpec(memory_space=pltpu.HBM)
    vmem = pl.BlockSpec(memory_space=pltpu.VMEM)
    home, total = pl.pallas_call(
        functools.partial(kernel, groups, freqs, zs, bins),
        out_shape=(
            jax.ShapeDtypeStruct((groups, rows, LANES), f32),
            jax.ShapeDtypeStruct((templates, LANES), f32),
        ),
        in_specs=[hbm, hbm, hbm],
        out_specs=(vmem, vmem),
        scratch_shapes=[
            pltpu.VMEM((all_rows, LANES), emission.dtype),
            pltpu.VMEM((all_rows, LANES), f32),
            pltpu.VMEM((step_weights.shape[1], step_weights.shape[0]), f32),
            pltpu.SMEM(template_ids.shape, jnp.int32),
            pltpu.VMEM((groups, rows + 1, LANES), f32),
            pltpu.VMEM((groups, rows + 1, LANES), f32),
            pltpu.VMEM((groups, 1, LANES), f32),
            pltpu.VMEM((2, 2, 1, LANES), f32),
            pltpu.VMEM((2, 2, 1, LANES), f32),
            pltpu.VMEM((groups, rows, LANES), f32),
            pltpu.VMEM((1, LANES), f32),
            pltpu.VMEM((groups // 2, 1, LANES), f32),
            pltpu.VMEM((1, LANES), f32),
            pltpu.VMEM((zs, 1, LANES), f32),
            pltpu.VMEM((1, LANES), f32),
            pltpu.VMEM((2 * xs, 1, LANES), f32),
            dma((3,)), dma((1,)), dma((1,)), dma((2,)), dma((2,)), dma((2, 2)), dma((1,)), dma((1,)), dma((1,)),
            dma((1,)), dma((1,)), dma((1,)), dma((1,)), dma((1,)), dma((1,)), dma((2,)),
        ],
        compiler_params=pltpu.CompilerParams(
            collective_id=0, has_side_effects=True, vmem_limit_bytes=32 * 1024 * 1024
        ),
    )(*(pltpu.with_memory_space_constraint(v, pltpu.HBM) for v in (lines, step_weights.T, template_ids)))
    anywhere = pl.BlockSpec(memory_space=pl.ANY)
    post, level = pl.pallas_call(
        functools.partial(finish, bins),
        out_shape=(
            jax.ShapeDtypeStruct((all_rows, LANES), f32),
            jax.ShapeDtypeStruct((templates,), f32),
        ),
        in_specs=[vmem, vmem],
        out_specs=(anywhere, anywhere),
        scratch_shapes=[pltpu.VMEM((all_rows, LANES), f32), pltpu.SMEM((templates,), f32), dma((groups // 2 + 1,))],
        compiler_params=pltpu.CompilerParams(vmem_limit_bytes=4 * 1024 * 1024),
    )(home, total)
    posterior = post.reshape(total_rows, templates, LANES).transpose(1, 0, 2).reshape(1, templates, here)
    return posterior, level


def solution(mesh):
    groups, freqs = mesh.shape["tm"], mesh.shape["freq"]
    zs = min(Z_CHIPS, freqs // 2)

    def whole(emission, step_weights, template_ids):
        return jax.shard_map(
            functools.partial(body, emission.shape[2], groups, freqs, zs),
            mesh=mesh,
            in_specs=(P("tm", None, "freq"), P(), P()),
            out_specs=(P("tm", None, "freq"), P()),
            check_vma=False,
        )(emission, step_weights, template_ids)

    return whole
```

```python
import functools

import jax
import jax.numpy as jnp
from jax import lax
from jax.experimental import pallas as pl
from jax.experimental.pallas import tpu as pltpu
from jax.sharding import PartitionSpec as P

MESH = pl.DeviceIdType.MESH
Z_CHIPS = 8
LANES = 128
TAIL = 8


def ring_order(chips):
    steps = [chips // 2]
    for d in range(chips // 2 - 1, 0, -1):
        steps += [-d, d]
    return [(d, c) for d in steps for c in (0, 1)] + [(0, 1)]


def kernel(groups, freqs, zs, bins, x_hbm, w_hbm, ids_hbm, home, total_ref,
           x_half, x_full, w_ref, ids_ref, stage, recv, halo, edge, beside, work,
           part, part_in, z_part, z_in, x_part, x_in,
           load_sem, send_sem, recv_sem, edge_send, edge_recv, halo_send, halo_recv, back_send, back_recv,
           part_send, part_recv, z_send, z_recv, x_send, x_recv, own_sem):
    xs = freqs // zs
    chips = groups // 2
    tm = lax.axis_index("tm")
    fq = lax.axis_index("freq")
    yi = tm // 2
    core = lax.rem(tm, 2)
    xi = fq // zs
    zi = lax.rem(fq, zs)
    next_fq = lax.rem(fq + 1, freqs)
    prev_fq = lax.rem(fq + freqs - 1, freqs)
    all_rows = x_hbm.shape[0]
    rows = all_rows // groups
    last = groups - 1
    order = ring_order(chips)

    def member(k):
        return lax.rem(yi + k[0] + chips, chips) * 2 + lax.rem(core + k[1], 2)

    loads = [pltpu.make_async_copy(src, dst, load_sem.at[i])
             for i, (src, dst) in enumerate(((x_hbm, x_half), (w_hbm, w_ref), (ids_hbm, ids_ref)))]
    for copy in loads:
        copy.start()

    barrier = pltpu.get_barrier_semaphore()

    def greet(t, f):
        pl.semaphore_signal(barrier, inc=1, device_id=(t, f), device_id_type=MESH)

    def across_x(k):
        place = lax.rem(xi * 2 + core + k, 2 * xs)
        return place, (yi * 2 + lax.rem(place, 2), place // 2 * zs + zi)

    peers = [(min(abs(k[0]), chips - abs(k[0])), member(k), fq) for k in order]
    peers += [(min(k, zs - k), tm, xi * zs + lax.rem(zi + k, zs)) for k in range(1, zs)]
    peers += [(min(k // 2, xs - k // 2), *across_x(k)[1]) for k in range(1, 2 * xs)]
    for _, t, f in sorted(peers, key=lambda peer: -peer[0]):
        greet(t, f)
    has_next = fq < freqs - 1
    has_prev = fq > 0
    next_turns = has_next & (zi == zs - 1)
    prev_turns = has_prev & (zi == 0)
    low_halo = (yi == 0) & has_prev
    high_halo = (yi == chips - 1) & has_next

    @pl.when(next_turns)
    def _():
        greet(tm, next_fq)

    @pl.when(prev_turns)
    def _():
        greet(tm, prev_fq)

    loads[0].wait()
    for r in range(0, all_rows, 16):
        x_full[r:r + 16, :] = x_half[r:r + 16, :].astype(jnp.float32)
    low_lanes = lax.broadcasted_iota(jnp.int32, (1, LANES), 1) < LANES // 2
    nothing = jnp.zeros((1, LANES), jnp.float32)
    for o in range(chips):
        for p in range(2):
            first = 2 * o * rows + p
            for r in range(0, rows, 8):
                stage[2 * o + p, r:r + 8, :] = x_full[pl.ds(first + 2 * r, 8, stride=2), :]
            after = first + 2 * rows
            high = x_full[after:after + 1, :] if o < chips - 1 else nothing
            low = x_full[first - 2:first - 1, :] if o > 0 else nothing
            stage[2 * o + p, rows:rows + 1, :] = jnp.where(low_lanes, high, low)
    for p in range(2):
        edge[0, p] = x_full[all_rows - 2 + p:all_rows - 1 + p, :]
        edge[1, p] = x_full[p:p + 1, :]

    expected = (groups - 1) + (zs - 1) + (2 * xs - 1)
    pl.semaphore_wait(barrier, expected + next_turns.astype(jnp.int32) + prev_turns.astype(jnp.int32))

    def remote(src, dst, s_sem, r_sem, to):
        return pltpu.make_async_remote_copy(
            src_ref=src, dst_ref=dst, send_sem=s_sem, recv_sem=r_sem, device_id=to, device_id_type=MESH)

    def all_of(ref, count, sem):
        block = ref.at[pl.ds(0, count)]
        pltpu.make_async_copy(block, block, sem).wait()

    def out_copy(k):
        to = member(k)
        return remote(stage.at[to], recv.at[tm], send_sem.at[0], recv_sem.at[0], (to, fq))

    def edge_copy(side, to):
        return remote(edge.at[side], beside.at[side], edge_send.at[side], edge_recv.at[side], (tm, to))

    def halo_copy(side, p):
        owner = p if side == 0 else last - 1 + p
        to = jnp.where(tm == owner, owner + 1 - 2 * p, owner)
        return tm == owner, remote(
            beside.at[side, p], halo.at[tm], halo_send.at[side, p], halo_recv.at[0], (to, fq))

    def halo_pass(side):
        edge_copy(side, fq).wait_recv()
        for p in range(2):
            here, copy = halo_copy(side, p)

            @pl.when(here)
            def _():
                pltpu.make_async_copy(beside.at[side, p], halo.at[tm], halo_recv.at[0]).start()

            @pl.when(jnp.logical_not(here))
            def _():
                copy.start()

    def halo_sent(side):
        for p in range(2):
            here, copy = halo_copy(side, p)

            @pl.when(jnp.logical_not(here))
            def _():
                copy.wait_send()

    @pl.when(has_next)
    def _():
        edge_copy(0, next_fq).start()

    @pl.when(has_prev)
    def _():
        edge_copy(1, prev_fq).start()

    for k in order:
        out_copy(k).start()

    @pl.when(has_prev)
    def _():
        halo_pass(0)

    @pl.when(has_next)
    def _():
        halo_pass(1)

    own = pltpu.make_async_copy(stage.at[tm], recv.at[tm], own_sem.at[0])
    own.start()

    loads[1].wait()
    loads[2].wait()
    slot = lax.broadcasted_iota(jnp.int32, w_ref.shape, 1)
    weights = jnp.sum(jnp.where(slot == ids_ref[core], w_ref[...], 0.0), axis=1, keepdims=True)
    weights = weights / jnp.sum(weights, axis=0, keepdims=True)
    field = (rows + TAIL, LANES)
    staying, rising, falling = (jnp.broadcast_to(weights[i:i + 1, :], field) for i in range(3))
    lane = lax.broadcasted_iota(jnp.int32, field, 1)
    row_index = lax.broadcasted_iota(jnp.int32, field, 0)

    from_other = (high_halo & low_lanes) | (low_halo & jnp.logical_not(low_lanes))

    def emission_of(t):
        tail = jnp.where(from_other, halo[t], recv[t, rows:rows + 1, :])
        return jnp.concatenate([recv[t, 0:rows, :], jnp.broadcast_to(tail, (TAIL, LANES))], axis=0)

    def below(v):
        turned = pltpu.roll(v, 1, 1)
        return jnp.where(lane == 0, pltpu.roll(turned, 1, 0), turned)

    def above(v):
        turned = pltpu.roll(v, LANES - 1, 1)
        return jnp.where(lane == LANES - 1, pltpu.roll(turned, field[0] - 1, 0), turned)

    own.wait()
    all_of(recv, groups - 1, recv_sem.at[0])

    @pl.when(low_halo | high_halo)
    def _():
        all_of(halo, groups, halo_recv.at[0])

    world_low = (yi == 0) & (fq == 0)
    world_high = (yi == chips - 1) & (fq == freqs - 1)
    outside = ((row_index == rows) & world_high) | ((row_index > rows) & world_low)
    b = jnp.ones(field, jnp.float32)
    u = jnp.where(outside, 0.0, b)

    def forward(t, u):
        return emission_of(t) * (staying * u + rising * below(u) + falling * above(u))

    def backward(s, b):
        g = emission_of(s + 1) * b
        return staying * g + rising * above(g) + falling * below(g)

    half = groups // 2

    def early(step, fields):
        u, b = fields
        u = forward(step, u)
        b = backward(last - 1 - step, b)
        work[step] = u[:rows]
        work[last - 1 - step] = b[:rows]
        return u, b

    work[last] = b[:rows]
    u, b = lax.fori_loop(0, half - 1, early, (u, b))
    u = forward(half - 1, u)
    b = backward(half - 1, b)
    middle = u[:rows] * b[:rows]
    work[half - 1] = middle
    part[...] = jnp.sum(middle, axis=0, keepdims=True)

    def spread(src, dst, to_of, mine, count, s_sem, r_sem):
        for k in range(1, count):
            remote(src, dst.at[mine], s_sem.at[0], r_sem.at[0], to_of(k)).start()

    def gather(src, dst, to_of, mine, count, s_sem, r_sem):
        all_of(dst, count - 1, r_sem.at[0])
        value = src[...]
        for k in range(1, count):
            value = value + dst[lax.rem(mine + k, count)]
        return value

    y_ring = (lambda k: (lax.rem(yi + k, chips) * 2 + core, fq), yi, chips, part_send, part_recv)
    z_ring = (lambda k: (tm, xi * zs + lax.rem(zi + k, zs)), zi, zs, z_send, z_recv)
    x_ring = (lambda k: across_x(k)[1], xi * 2 + core, 2 * xs, x_send, x_recv)
    spread(part, part_in, *y_ring)

    def late(step, fields):
        u, b = fields
        u = forward(step, u)
        b = backward(last - 1 - step, b)
        work[step] = u[:rows] * work[step]
        work[last - 1 - step] = work[last - 1 - step] * b[:rows]
        return u, b

    u, _ = lax.fori_loop(half, last, late, (u, b))
    work[last] = forward(last, u)[:rows] * work[last]

    def back_copy(k):
        to = member(k)
        return remote(work.at[to], home.at[tm], back_send.at[0], back_recv.at[0], (to, fq))

    own_back = pltpu.make_async_copy(work.at[tm], home.at[tm], own_sem.at[1])
    own_back.start()
    for k in order[:len(order) // 2]:
        back_copy(k).start()

    z_part[...] = gather(part, part_in, *y_ring)
    spread(z_part, z_in, *z_ring)
    for k in order[len(order) // 2:]:
        back_copy(k).start()
    all_of(stage, groups - 1, send_sem.at[0])

    x_part[...] = gather(z_part, z_in, *z_ring)
    spread(x_part, x_in, *x_ring)

    @pl.when(has_next)
    def _():
        edge_copy(0, next_fq).wait_send()
        halo_sent(1)

    @pl.when(has_prev)
    def _():
        edge_copy(1, prev_fq).wait_send()
        halo_sent(0)

    all_of(part_in, chips - 1, part_send.at[0])
    all_of(z_in, zs - 1, z_send.at[0])
    all_of(x_in, 2 * xs - 1, x_recv.at[0])
    same = x_part[...]
    other = jnp.zeros_like(same)
    for k in range(1, 2 * xs):
        place, _ = across_x(k)
        if k % 2 == 0:
            same = same + x_in[place]
        else:
            other = other + x_in[place]
    for p in range(2):
        whole = jnp.sum(jnp.where(core == p, same, other), axis=1, keepdims=True)
        total_ref[p:p + 1, :] = jnp.broadcast_to(whole, (1, LANES))

    own_back.wait()
    all_of(home, groups - 1, back_recv.at[0])
    all_of(x_in, 2 * xs - 1, x_send.at[0])
    all_of(work, groups - 1, back_send.at[0])


def finish(bins, home, total_ref, out_hbm, level_hbm, out, level, sems):
    groups, rows = home.shape[0], home.shape[1]
    totals = [total_ref[p:p + 1, :] for p in range(2)]
    scales = [bins / total for total in totals]
    blocks = groups // 2
    copies = []
    for o in range(blocks):
        first = o * 2 * rows
        for p in range(2):
            for r in range(0, rows, 8):
                out[pl.ds(first + p + 2 * r, 8, stride=2), :] = home[2 * o + p, r:r + 8, :] * scales[p]
        block = pl.ds(first, 2 * rows)
        copies.append(pltpu.make_async_copy(out.at[block, :], out_hbm.at[block, :], sems.at[o]))
        copies[-1].start()
    for p in range(2):
        level[p] = (jnp.log(totals[p] * (1.0 / bins)) * (1.0 / groups))[0, 0]
    copies.append(pltpu.make_async_copy(level, level_hbm, sems.at[blocks]))
    copies[-1].start()
    for copy in copies:
        copy.wait()


def body(bins, groups, freqs, zs, emission, step_weights, template_ids):
    templates = emission.shape[1]
    here = emission.shape[2]
    total_rows = here // LANES
    all_rows = templates * total_rows
    rows = all_rows // groups
    xs = freqs // zs
    f32 = jnp.float32
    dma = pltpu.SemaphoreType.DMA
    lines = emission.reshape(templates, total_rows, LANES).transpose(1, 0, 2).reshape(all_rows, LANES)
    hbm = pl.BlockSpec(memory_space=pltpu.HBM)
    vmem = pl.BlockSpec(memory_space=pltpu.VMEM)
    home, total = pl.pallas_call(
        functools.partial(kernel, groups, freqs, zs, bins),
        out_shape=(
            jax.ShapeDtypeStruct((groups, rows, LANES), f32),
            jax.ShapeDtypeStruct((templates, LANES), f32),
        ),
        in_specs=[hbm, hbm, hbm],
        out_specs=(vmem, vmem),
        scratch_shapes=[
            pltpu.VMEM((all_rows, LANES), emission.dtype),
            pltpu.VMEM((all_rows, LANES), f32),
            pltpu.VMEM((step_weights.shape[1], step_weights.shape[0]), f32),
            pltpu.SMEM(template_ids.shape, jnp.int32),
            pltpu.VMEM((groups, rows + 1, LANES), f32),
            pltpu.VMEM((groups, rows + 1, LANES), f32),
            pltpu.VMEM((groups, 1, LANES), f32),
            pltpu.VMEM((2, 2, 1, LANES), f32),
            pltpu.VMEM((2, 2, 1, LANES), f32),
            pltpu.VMEM((groups, rows, LANES), f32),
            pltpu.VMEM((1, LANES), f32),
            pltpu.VMEM((groups // 2, 1, LANES), f32),
            pltpu.VMEM((1, LANES), f32),
            pltpu.VMEM((zs, 1, LANES), f32),
            pltpu.VMEM((1, LANES), f32),
            pltpu.VMEM((2 * xs, 1, LANES), f32),
            dma((3,)), dma((1,)), dma((1,)), dma((2,)), dma((2,)), dma((2, 2)), dma((1,)), dma((1,)), dma((1,)),
            dma((1,)), dma((1,)), dma((1,)), dma((1,)), dma((1,)), dma((1,)), dma((2,)),
        ],
        compiler_params=pltpu.CompilerParams(
            collective_id=0, has_side_effects=True, vmem_limit_bytes=32 * 1024 * 1024
        ),
    )(*(pltpu.with_memory_space_constraint(v, pltpu.HBM) for v in (lines, step_weights.T, template_ids)))
    anywhere = pl.BlockSpec(memory_space=pl.ANY)
    post, level = pl.pallas_call(
        functools.partial(finish, bins),
        out_shape=(
            jax.ShapeDtypeStruct((all_rows, LANES), f32),
            jax.ShapeDtypeStruct((templates,), f32),
        ),
        in_specs=[vmem, vmem],
        out_specs=(anywhere, anywhere),
        scratch_shapes=[pltpu.VMEM((all_rows, LANES), f32), pltpu.SMEM((templates,), f32), dma((groups // 2 + 1,))],
        compiler_params=pltpu.CompilerParams(vmem_limit_bytes=4 * 1024 * 1024),
    )(home, total)
    posterior = post.reshape(total_rows, templates, LANES).transpose(1, 0, 2).reshape(1, templates, here)
    return posterior, level


def solution(mesh):
    groups, freqs = mesh.shape["tm"], mesh.shape["freq"]
    zs = min(Z_CHIPS, freqs // 2)

    def whole(emission, step_weights, template_ids):
        return jax.shard_map(
            functools.partial(body, emission.shape[2], groups, freqs, zs),
            mesh=mesh,
            in_specs=(P("tm", None, "freq"), P(), P()),
            out_specs=(P("tm", None, "freq"), P()),
            check_vma=False,
        )(emission, step_weights, template_ids)

    return whole
```

```python
import functools

import jax
import jax.numpy as jnp
from jax import lax
from jax.experimental import pallas as pl
from jax.experimental.pallas import tpu as pltpu
from jax.sharding import PartitionSpec as P

MESH = pl.DeviceIdType.MESH
Z_CHIPS = 8
LANES = 128
TAIL = 8


def ring_order(chips):
    steps = [chips // 2]
    for d in range(chips // 2 - 1, 0, -1):
        steps += [-d, d]
    return [(d, c) for d in steps for c in (0, 1)] + [(0, 1)]


def loop(count, step):
    lax.fori_loop(0, count, lambda i, c: (step(i), c)[1], 0)


def kernel(groups, freqs, zs, bins, x_hbm, w_hbm, ids_hbm, home, total_ref,
           x_half, x_full, w_ref, ids_ref, stage, recv, halo, edge, beside, work,
           part, part_in, z_part, z_in, x_part, x_in,
           load_sem, send_sem, recv_sem, edge_send, edge_recv, halo_send, halo_recv, back_send, back_recv,
           part_send, part_recv, z_send, z_recv, x_send, x_recv, own_sem):
    xs = freqs // zs
    chips = groups // 2
    tm = lax.axis_index("tm")
    fq = lax.axis_index("freq")
    yi = tm // 2
    core = lax.rem(tm, 2)
    xi = fq // zs
    zi = lax.rem(fq, zs)
    next_fq = lax.rem(fq + 1, freqs)
    prev_fq = lax.rem(fq + freqs - 1, freqs)
    all_rows = x_hbm.shape[0]
    rows = all_rows // groups
    last = groups - 1
    order = ring_order(chips)

    def member(k):
        return lax.rem(yi + k[0] + chips, chips) * 2 + lax.rem(core + k[1], 2)

    loads = [pltpu.make_async_copy(src, dst, load_sem.at[i])
             for i, (src, dst) in enumerate(((x_hbm, x_half), (w_hbm, w_ref), (ids_hbm, ids_ref)))]
    for copy in loads:
        copy.start()

    barrier = pltpu.get_barrier_semaphore()

    def greet(t, f):
        pl.semaphore_signal(barrier, inc=1, device_id=(t, f), device_id_type=MESH)

    def across_x(k):
        place = lax.rem(xi * 2 + core + k, 2 * xs)
        return place, (yi * 2 + lax.rem(place, 2), place // 2 * zs + zi)

    peers = [(min(abs(k[0]), chips - abs(k[0])), member(k), fq) for k in order]
    peers += [(min(k, zs - k), tm, xi * zs + lax.rem(zi + k, zs)) for k in range(1, zs)]
    peers += [(min(k // 2, xs - k // 2), *across_x(k)[1]) for k in range(1, 2 * xs)]
    for _, t, f in sorted(peers, key=lambda peer: -peer[0]):
        greet(t, f)
    has_next = fq < freqs - 1
    has_prev = fq > 0
    next_turns = has_next & (zi == zs - 1)
    prev_turns = has_prev & (zi == 0)
    low_halo = (yi == 0) & has_prev
    high_halo = (yi == chips - 1) & has_next

    @pl.when(next_turns)
    def _():
        greet(tm, next_fq)

    @pl.when(prev_turns)
    def _():
        greet(tm, prev_fq)

    loads[0].wait()
    low_lanes = lax.broadcasted_iota(jnp.int32, (1, LANES), 1) < LANES // 2

    def widen(o):
        block = pl.ds(pl.multiple_of(o * 2 * rows, 2 * rows), 2 * rows)
        x_full[block, :] = x_half[block, :].astype(jnp.float32)

    def stage_one(o):
        for p in range(2):
            first = o * 2 * rows + p
            for r in range(0, rows, 8):
                stage[2 * o + p, r:r + 8, :] = x_full[pl.ds(first + 2 * r, 8, stride=2), :]
            high = x_full[pl.ds(jnp.minimum(first + 2 * rows, all_rows - 2 + p), 1), :]
            low = x_full[pl.ds(jnp.maximum(first - 2, p), 1), :]
            stage[2 * o + p, rows:rows + 1, :] = jnp.where(
                low_lanes, jnp.where(o < chips - 1, high, 0.0), jnp.where(o > 0, low, 0.0))

    loop(chips, widen)
    loop(chips, stage_one)
    for p in range(2):
        edge[0, p] = x_full[all_rows - 2 + p:all_rows - 1 + p, :]
        edge[1, p] = x_full[p:p + 1, :]

    expected = (groups - 1) + (zs - 1) + (2 * xs - 1)
    pl.semaphore_wait(barrier, expected + next_turns.astype(jnp.int32) + prev_turns.astype(jnp.int32))

    def remote(src, dst, s_sem, r_sem, to):
        return pltpu.make_async_remote_copy(
            src_ref=src, dst_ref=dst, send_sem=s_sem, recv_sem=r_sem, device_id=to, device_id_type=MESH)

    def all_of(ref, count, sem):
        block = ref.at[pl.ds(0, count)]
        pltpu.make_async_copy(block, block, sem).wait()

    def out_copy(k):
        to = member(k)
        return remote(stage.at[to], recv.at[tm], send_sem.at[0], recv_sem.at[0], (to, fq))

    def edge_copy(side, to):
        return remote(edge.at[side], beside.at[side], edge_send.at[side], edge_recv.at[side], (tm, to))

    def halo_copy(side, p):
        owner = p if side == 0 else last - 1 + p
        to = jnp.where(tm == owner, owner + 1 - 2 * p, owner)
        return tm == owner, remote(
            beside.at[side, p], halo.at[tm], halo_send.at[side, p], halo_recv.at[0], (to, fq))

    def halo_pass(side):
        edge_copy(side, fq).wait_recv()
        for p in range(2):
            here, copy = halo_copy(side, p)

            @pl.when(here)
            def _():
                pltpu.make_async_copy(beside.at[side, p], halo.at[tm], halo_recv.at[0]).start()

            @pl.when(jnp.logical_not(here))
            def _():
                copy.start()

    def halo_sent(side):
        for p in range(2):
            here, copy = halo_copy(side, p)

            @pl.when(jnp.logical_not(here))
            def _():
                copy.wait_send()

    @pl.when(has_next)
    def _():
        edge_copy(0, next_fq).start()

    @pl.when(has_prev)
    def _():
        edge_copy(1, prev_fq).start()

    for k in order:
        out_copy(k).start()

    @pl.when(has_prev)
    def _():
        halo_pass(0)

    @pl.when(has_next)
    def _():
        halo_pass(1)

    own = pltpu.make_async_copy(stage.at[tm], recv.at[tm], own_sem.at[0])
    own.start()

    loads[1].wait()
    loads[2].wait()
    slot = lax.broadcasted_iota(jnp.int32, w_ref.shape, 1)
    weights = jnp.sum(jnp.where(slot == ids_ref[core], w_ref[...], 0.0), axis=1, keepdims=True)
    weights = weights / jnp.sum(weights, axis=0, keepdims=True)
    field = (rows + TAIL, LANES)
    staying, rising, falling = (jnp.broadcast_to(weights[i:i + 1, :], field) for i in range(3))
    lane = lax.broadcasted_iota(jnp.int32, field, 1)
    row_index = lax.broadcasted_iota(jnp.int32, field, 0)

    from_other = (high_halo & low_lanes) | (low_halo & jnp.logical_not(low_lanes))

    def emission_of(t):
        tail = jnp.where(from_other, halo[t], recv[t, rows:rows + 1, :])
        return jnp.concatenate([recv[t, 0:rows, :], jnp.broadcast_to(tail, (TAIL, LANES))], axis=0)

    def below(v):
        turned = pltpu.roll(v, 1, 1)
        return jnp.where(lane == 0, pltpu.roll(turned, 1, 0), turned)

    def above(v):
        turned = pltpu.roll(v, LANES - 1, 1)
        return jnp.where(lane == LANES - 1, pltpu.roll(turned, field[0] - 1, 0), turned)

    own.wait()
    all_of(recv, groups - 1, recv_sem.at[0])

    @pl.when(low_halo | high_halo)
    def _():
        all_of(halo, groups, halo_recv.at[0])

    world_low = (yi == 0) & (fq == 0)
    world_high = (yi == chips - 1) & (fq == freqs - 1)
    outside = ((row_index == rows) & world_high) | ((row_index > rows) & world_low)
    b = jnp.ones(field, jnp.float32)
    u = jnp.where(outside, 0.0, b)

    def forward(t, u):
        return emission_of(t) * (staying * u + rising * below(u) + falling * above(u))

    def backward(s, b):
        g = emission_of(s + 1) * b
        return staying * g + rising * above(g) + falling * below(g)

    half = groups // 2

    def early(step, fields):
        u, b = fields
        u = forward(step, u)
        b = backward(last - 1 - step, b)
        work[step] = u[:rows]
        work[last - 1 - step] = b[:rows]
        return u, b

    work[last] = b[:rows]
    u, b = lax.fori_loop(0, half - 1, early, (u, b))
    u = forward(half - 1, u)
    b = backward(half - 1, b)
    middle = u[:rows] * b[:rows]
    work[half - 1] = middle
    part[...] = jnp.sum(middle, axis=0, keepdims=True)

    def spread(src, dst, to_of, mine, count, s_sem, r_sem):
        for k in range(1, count):
            remote(src, dst.at[mine], s_sem.at[0], r_sem.at[0], to_of(k)).start()

    def gather(src, dst, to_of, mine, count, s_sem, r_sem):
        all_of(dst, count - 1, r_sem.at[0])
        value = src[...]
        for k in range(1, count):
            value = value + dst[lax.rem(mine + k, count)]
        return value

    y_ring = (lambda k: (lax.rem(yi + k, chips) * 2 + core, fq), yi, chips, part_send, part_recv)
    z_ring = (lambda k: (tm, xi * zs + lax.rem(zi + k, zs)), zi, zs, z_send, z_recv)
    x_ring = (lambda k: across_x(k)[1], xi * 2 + core, 2 * xs, x_send, x_recv)
    spread(part, part_in, *y_ring)

    def late(step, fields):
        u, b = fields
        u = forward(step, u)
        b = backward(last - 1 - step, b)
        work[step] = u[:rows] * work[step]
        work[last - 1 - step] = work[last - 1 - step] * b[:rows]
        return u, b

    u, _ = lax.fori_loop(half, last, late, (u, b))
    work[last] = forward(last, u)[:rows] * work[last]

    def back_copy(k):
        to = member(k)
        return remote(work.at[to], home.at[tm], back_send.at[0], back_recv.at[0], (to, fq))

    own_back = pltpu.make_async_copy(work.at[tm], home.at[tm], own_sem.at[1])
    own_back.start()
    for k in order[:len(order) // 2]:
        back_copy(k).start()

    z_part[...] = gather(part, part_in, *y_ring)
    spread(z_part, z_in, *z_ring)
    for k in order[len(order) // 2:]:
        back_copy(k).start()
    all_of(stage, groups - 1, send_sem.at[0])

    x_part[...] = gather(z_part, z_in, *z_ring)
    spread(x_part, x_in, *x_ring)

    @pl.when(has_next)
    def _():
        edge_copy(0, next_fq).wait_send()
        halo_sent(1)

    @pl.when(has_prev)
    def _():
        edge_copy(1, prev_fq).wait_send()
        halo_sent(0)

    all_of(part_in, chips - 1, part_send.at[0])
    all_of(z_in, zs - 1, z_send.at[0])
    all_of(x_in, 2 * xs - 1, x_recv.at[0])
    same = x_part[...]
    other = jnp.zeros_like(same)
    for k in range(1, 2 * xs):
        place, _ = across_x(k)
        if k % 2 == 0:
            same = same + x_in[place]
        else:
            other = other + x_in[place]
    for p in range(2):
        whole = jnp.sum(jnp.where(core == p, same, other), axis=1, keepdims=True)
        total_ref[p:p + 1, :] = jnp.broadcast_to(whole, (1, LANES))

    own_back.wait()
    all_of(home, groups - 1, back_recv.at[0])
    all_of(x_in, 2 * xs - 1, x_send.at[0])
    all_of(work, groups - 1, back_send.at[0])


def finish(bins, home, total_ref, out_hbm, level_hbm, out, level, sems):
    groups, rows = home.shape[0], home.shape[1]
    totals = [total_ref[p:p + 1, :] for p in range(2)]
    scales = [bins / total for total in totals]

    def hand_out(o):
        first = pl.multiple_of(o * 2 * rows, 2 * rows)
        for p in range(2):
            for r in range(0, rows, 8):
                out[pl.ds(first + p + 2 * r, 8, stride=2), :] = home[2 * o + p, r:r + 8, :] * scales[p]
        block = pl.ds(first, 2 * rows)
        pltpu.make_async_copy(out.at[block, :], out_hbm.at[block, :], sems.at[0]).start()

    loop(groups // 2, hand_out)
    for p in range(2):
        level[p] = (jnp.log(totals[p] * (1.0 / bins)) * (1.0 / groups))[0, 0]
    level_copy = pltpu.make_async_copy(level, level_hbm, sems.at[1])
    level_copy.start()
    pltpu.make_async_copy(out, out_hbm, sems.at[0]).wait()
    level_copy.wait()


def body(bins, groups, freqs, zs, emission, step_weights, template_ids):
    templates = emission.shape[1]
    here = emission.shape[2]
    total_rows = here // LANES
    all_rows = templates * total_rows
    rows = all_rows // groups
    xs = freqs // zs
    f32 = jnp.float32
    dma = pltpu.SemaphoreType.DMA
    lines = emission.reshape(templates, total_rows, LANES).transpose(1, 0, 2).reshape(all_rows, LANES)
    hbm = pl.BlockSpec(memory_space=pltpu.HBM)
    vmem = pl.BlockSpec(memory_space=pltpu.VMEM)
    home, total = pl.pallas_call(
        functools.partial(kernel, groups, freqs, zs, bins),
        out_shape=(
            jax.ShapeDtypeStruct((groups, rows, LANES), f32),
            jax.ShapeDtypeStruct((templates, LANES), f32),
        ),
        in_specs=[hbm, hbm, hbm],
        out_specs=(vmem, vmem),
        scratch_shapes=[
            pltpu.VMEM((all_rows, LANES), emission.dtype),
            pltpu.VMEM((all_rows, LANES), f32),
            pltpu.VMEM((step_weights.shape[1], step_weights.shape[0]), f32),
            pltpu.SMEM(template_ids.shape, jnp.int32),
            pltpu.VMEM((groups, rows + 1, LANES), f32),
            pltpu.VMEM((groups, rows + 1, LANES), f32),
            pltpu.VMEM((groups, 1, LANES), f32),
            pltpu.VMEM((2, 2, 1, LANES), f32),
            pltpu.VMEM((2, 2, 1, LANES), f32),
            pltpu.VMEM((groups, rows, LANES), f32),
            pltpu.VMEM((1, LANES), f32),
            pltpu.VMEM((groups // 2, 1, LANES), f32),
            pltpu.VMEM((1, LANES), f32),
            pltpu.VMEM((zs, 1, LANES), f32),
            pltpu.VMEM((1, LANES), f32),
            pltpu.VMEM((2 * xs, 1, LANES), f32),
            dma((3,)), dma((1,)), dma((1,)), dma((2,)), dma((2,)), dma((2, 2)), dma((1,)), dma((1,)), dma((1,)),
            dma((1,)), dma((1,)), dma((1,)), dma((1,)), dma((1,)), dma((1,)), dma((2,)),
        ],
        compiler_params=pltpu.CompilerParams(
            collective_id=0, has_side_effects=True, vmem_limit_bytes=32 * 1024 * 1024
        ),
    )(*(pltpu.with_memory_space_constraint(v, pltpu.HBM) for v in (lines, step_weights.T, template_ids)))
    anywhere = pl.BlockSpec(memory_space=pl.ANY)
    post, level = pl.pallas_call(
        functools.partial(finish, bins),
        out_shape=(
            jax.ShapeDtypeStruct((all_rows, LANES), f32),
            jax.ShapeDtypeStruct((templates,), f32),
        ),
        in_specs=[vmem, vmem],
        out_specs=(anywhere, anywhere),
        scratch_shapes=[pltpu.VMEM((all_rows, LANES), f32), pltpu.SMEM((templates,), f32), dma((2,))],
        compiler_params=pltpu.CompilerParams(vmem_limit_bytes=4 * 1024 * 1024),
    )(home, total)
    posterior = post.reshape(total_rows, templates, LANES).transpose(1, 0, 2).reshape(1, templates, here)
    return posterior, level


def solution(mesh):
    groups, freqs = mesh.shape["tm"], mesh.shape["freq"]
    zs = min(Z_CHIPS, freqs // 2)

    def whole(emission, step_weights, template_ids):
        return jax.shard_map(
            functools.partial(body, emission.shape[2], groups, freqs, zs),
            mesh=mesh,
            in_specs=(P("tm", None, "freq"), P(), P()),
            out_specs=(P("tm", None, "freq"), P()),
            check_vma=False,
        )(emission, step_weights, template_ids)

    return whole
```

```python
import functools

import jax
import jax.numpy as jnp
from jax import lax
from jax.experimental import pallas as pl
from jax.experimental.pallas import tpu as pltpu
from jax.sharding import PartitionSpec as P

MESH = pl.DeviceIdType.MESH
Z_CHIPS = 8
LANES = 128
TAIL = 8


def ring_order(chips):
    steps = [chips // 2]
    for d in range(chips // 2 - 1, 0, -1):
        steps += [-d, d]
    return [(d, c) for d in steps for c in (0, 1)] + [(0, 1)]


def loop(count, step):
    lax.fori_loop(0, count, lambda i, c: (step(i), c)[1], 0)


def kernel(groups, freqs, zs, bins, x_hbm, w_hbm, ids_hbm, home, total_ref,
           x_half, x_full, w_ref, ids_ref, stage, recv, halo, edge, beside, work,
           part, part_in, z_part, z_in, x_part, x_in,
           load_sem, send_sem, recv_sem, edge_send, edge_recv, halo_send, halo_recv, back_send, back_recv,
           part_send, part_recv, z_send, z_recv, x_send, x_recv, own_sem):
    xs = freqs // zs
    chips = groups // 2
    tm = lax.axis_index("tm")
    fq = lax.axis_index("freq")
    yi = tm // 2
    core = lax.rem(tm, 2)
    xi = fq // zs
    zi = lax.rem(fq, zs)
    next_fq = lax.rem(fq + 1, freqs)
    prev_fq = lax.rem(fq + freqs - 1, freqs)
    all_rows = x_hbm.shape[0]
    rows = all_rows // groups
    last = groups - 1
    order = ring_order(chips)

    def member(k):
        return lax.rem(yi + k[0] + chips, chips) * 2 + lax.rem(core + k[1], 2)

    loads = [pltpu.make_async_copy(src, dst, load_sem.at[i])
             for i, (src, dst) in enumerate(((x_hbm, x_half), (w_hbm, w_ref), (ids_hbm, ids_ref)))]
    for copy in loads:
        copy.start()

    barrier = pltpu.get_barrier_semaphore()

    def greet(t, f):
        pl.semaphore_signal(barrier, inc=1, device_id=(t, f), device_id_type=MESH)

    def across_x(k):
        place = lax.rem(xi * 2 + core + k, 2 * xs)
        return place, (yi * 2 + lax.rem(place, 2), place // 2 * zs + zi)

    peers = [(min(abs(k[0]), chips - abs(k[0])), member(k), fq) for k in order]
    peers += [(min(k, zs - k), tm, xi * zs + lax.rem(zi + k, zs)) for k in range(1, zs)]
    peers += [(min(k // 2, xs - k // 2), *across_x(k)[1]) for k in range(1, 2 * xs)]
    for _, t, f in sorted(peers, key=lambda peer: -peer[0]):
        greet(t, f)
    has_next = fq < freqs - 1
    has_prev = fq > 0
    next_turns = has_next & (zi == zs - 1)
    prev_turns = has_prev & (zi == 0)
    low_halo = (yi == 0) & has_prev
    high_halo = (yi == chips - 1) & has_next

    @pl.when(next_turns)
    def _():
        greet(tm, next_fq)

    @pl.when(prev_turns)
    def _():
        greet(tm, prev_fq)

    loads[0].wait()
    low_lanes = lax.broadcasted_iota(jnp.int32, (1, LANES), 1) < LANES // 2

    def widen(o):
        block = pl.ds(pl.multiple_of(o * 2 * rows, 2 * rows), 2 * rows)
        x_full[block, :] = x_half[block, :].astype(jnp.float32)

    def stage_one(o):
        for p in range(2):
            first = o * 2 * rows + p
            for r in range(0, rows, 8):
                stage[2 * o + p, r:r + 8, :] = x_full[pl.ds(first + 2 * r, 8, stride=2), :]
            high = x_full[pl.ds(jnp.minimum(first + 2 * rows, all_rows - 2 + p), 1), :]
            low = x_full[pl.ds(jnp.maximum(first - 2, p), 1), :]
            stage[2 * o + p, rows:rows + 1, :] = jnp.where(
                low_lanes, jnp.where(o < chips - 1, high, 0.0), jnp.where(o > 0, low, 0.0))

    loop(chips, widen)
    loop(chips, stage_one)
    for p in range(2):
        edge[0, p] = x_full[all_rows - 2 + p:all_rows - 1 + p, :]
        edge[1, p] = x_full[p:p + 1, :]

    expected = (groups - 1) + (zs - 1) + (2 * xs - 1)
    pl.semaphore_wait(barrier, expected + next_turns.astype(jnp.int32) + prev_turns.astype(jnp.int32))

    def remote(src, dst, s_sem, r_sem, to):
        return pltpu.make_async_remote_copy(
            src_ref=src, dst_ref=dst, send_sem=s_sem, recv_sem=r_sem, device_id=to, device_id_type=MESH)

    def all_of(ref, count, sem):
        block = ref.at[pl.ds(0, count)]
        pltpu.make_async_copy(block, block, sem).wait()

    def out_copy(k):
        to = member(k)
        return remote(stage.at[to], recv.at[tm], send_sem.at[0], recv_sem.at[0], (to, fq))

    def edge_copy(side, to):
        return remote(edge.at[side], beside.at[side], edge_send.at[side], edge_recv.at[side], (tm, to))

    def halo_copy(side, p):
        owner = p if side == 0 else last - 1 + p
        to = jnp.where(tm == owner, owner + 1 - 2 * p, owner)
        return tm == owner, remote(
            beside.at[side, p], halo.at[tm], halo_send.at[side, p], halo_recv.at[0], (to, fq))

    def halo_pass(side):
        edge_copy(side, fq).wait_recv()
        for p in range(2):
            here, copy = halo_copy(side, p)

            @pl.when(here)
            def _():
                pltpu.make_async_copy(beside.at[side, p], halo.at[tm], halo_recv.at[0]).start()

            @pl.when(jnp.logical_not(here))
            def _():
                copy.start()

    def halo_sent(side):
        for p in range(2):
            here, copy = halo_copy(side, p)

            @pl.when(jnp.logical_not(here))
            def _():
                copy.wait_send()

    @pl.when(has_next)
    def _():
        edge_copy(0, next_fq).start()

    @pl.when(has_prev)
    def _():
        edge_copy(1, prev_fq).start()

    for k in order:
        out_copy(k).start()

    @pl.when(has_prev)
    def _():
        halo_pass(0)

    @pl.when(has_next)
    def _():
        halo_pass(1)

    own = pltpu.make_async_copy(stage.at[tm], recv.at[tm], own_sem.at[0])
    own.start()

    loads[1].wait()
    loads[2].wait()
    slot = lax.broadcasted_iota(jnp.int32, w_ref.shape, 1)
    weights = jnp.sum(jnp.where(slot == ids_ref[core], w_ref[...], 0.0), axis=1, keepdims=True)
    weights = weights / jnp.sum(weights, axis=0, keepdims=True)
    field = (rows + TAIL, LANES)
    staying, rising, falling = (jnp.broadcast_to(weights[i:i + 1, :], field) for i in range(3))
    lane = lax.broadcasted_iota(jnp.int32, field, 1)
    row_index = lax.broadcasted_iota(jnp.int32, field, 0)

    from_other = (high_halo & low_lanes) | (low_halo & jnp.logical_not(low_lanes))

    def emission_of(t):
        tail = jnp.where(from_other, halo[t], recv[t, rows:rows + 1, :])
        return jnp.concatenate([recv[t, 0:rows, :], jnp.broadcast_to(tail, (TAIL, LANES))], axis=0)

    def below(v):
        turned = pltpu.roll(v, 1, 1)
        return jnp.where(lane == 0, pltpu.roll(turned, 1, 0), turned)

    def above(v):
        turned = pltpu.roll(v, LANES - 1, 1)
        return jnp.where(lane == LANES - 1, pltpu.roll(turned, field[0] - 1, 0), turned)

    own.wait()
    all_of(recv, groups - 1, recv_sem.at[0])

    @pl.when(low_halo | high_halo)
    def _():
        all_of(halo, groups, halo_recv.at[0])

    world_low = (yi == 0) & (fq == 0)
    world_high = (yi == chips - 1) & (fq == freqs - 1)
    outside = ((row_index == rows) & world_high) | ((row_index > rows) & world_low)
    b = jnp.ones(field, jnp.float32)
    u = jnp.where(outside, 0.0, b)

    def forward(t, u):
        return emission_of(t) * (staying * u + rising * below(u) + falling * above(u))

    def backward(s, b):
        g = emission_of(s + 1) * b
        return staying * g + rising * above(g) + falling * below(g)

    half = groups // 2

    def early(step, fields):
        u, b = fields
        u = forward(step, u)
        b = backward(last - 1 - step, b)
        work[step] = u[:rows]
        work[last - 1 - step] = b[:rows]
        return u, b

    work[last] = b[:rows]
    u, b = lax.fori_loop(0, half - 1, early, (u, b))
    u = forward(half - 1, u)
    b = backward(half - 1, b)
    middle = u[:rows] * b[:rows]
    work[half - 1] = middle
    part[...] = jnp.sum(middle, axis=0, keepdims=True)

    def spread(src, dst, to_of, mine, count, s_sem, r_sem):
        for k in range(1, count):
            remote(src, dst.at[mine], s_sem.at[0], r_sem.at[0], to_of(k)).start()

    def tree_sum(values):
        while len(values) > 1:
            values = [sum(values[i:i + 2]) for i in range(0, len(values), 2)]
        return values[0]

    def gather(src, dst, to_of, mine, count, s_sem, r_sem):
        dst[mine] = src[...]
        all_of(dst, count - 1, r_sem.at[0])

    y_ring = (lambda k: (lax.rem(yi + k, chips) * 2 + core, fq), yi, chips, part_send, part_recv)
    z_ring = (lambda k: (tm, xi * zs + lax.rem(zi + k, zs)), zi, zs, z_send, z_recv)
    x_ring = (lambda k: across_x(k)[1], xi * 2 + core, 2 * xs, x_send, x_recv)
    spread(part, part_in, *y_ring)

    def late(step, fields):
        u, b = fields
        u = forward(step, u)
        b = backward(last - 1 - step, b)
        work[step] = u[:rows] * work[step]
        work[last - 1 - step] = work[last - 1 - step] * b[:rows]
        return u, b

    u, _ = lax.fori_loop(half, last, late, (u, b))
    work[last] = forward(last, u)[:rows] * work[last]

    def back_copy(k):
        to = member(k)
        return remote(work.at[to], home.at[tm], back_send.at[0], back_recv.at[0], (to, fq))

    own_back = pltpu.make_async_copy(work.at[tm], home.at[tm], own_sem.at[1])
    own_back.start()
    for k in order[:len(order) // 2]:
        back_copy(k).start()

    gather(part, part_in, *y_ring)
    z_part[...] = tree_sum([part_in[i] for i in range(chips)])
    spread(z_part, z_in, *z_ring)
    for k in order[len(order) // 2:]:
        back_copy(k).start()
    all_of(stage, groups - 1, send_sem.at[0])

    gather(z_part, z_in, *z_ring)
    x_part[...] = tree_sum([z_in[i] for i in range(zs)])
    spread(x_part, x_in, *x_ring)

    @pl.when(has_next)
    def _():
        edge_copy(0, next_fq).wait_send()
        halo_sent(1)

    @pl.when(has_prev)
    def _():
        edge_copy(1, prev_fq).wait_send()
        halo_sent(0)

    all_of(part_in, chips - 1, part_send.at[0])
    all_of(z_in, zs - 1, z_send.at[0])
    gather(x_part, x_in, *x_ring)
    for p in range(2):
        whole = jnp.sum(tree_sum([x_in[2 * i + p] for i in range(xs)]), axis=1, keepdims=True)
        total_ref[p:p + 1, :] = jnp.broadcast_to(whole, (1, LANES))

    own_back.wait()
    all_of(home, groups - 1, back_recv.at[0])
    all_of(x_in, 2 * xs - 1, x_send.at[0])
    all_of(work, groups - 1, back_send.at[0])


def finish(bins, home, total_ref, out_hbm, level_hbm, out, level, sems):
    groups, rows = home.shape[0], home.shape[1]
    totals = [total_ref[p:p + 1, :] for p in range(2)]
    scales = [bins / total for total in totals]

    def hand_out(o):
        first = pl.multiple_of(o * 2 * rows, 2 * rows)
        for p in range(2):
            for r in range(0, rows, 8):
                out[pl.ds(first + p + 2 * r, 8, stride=2), :] = home[2 * o + p, r:r + 8, :] * scales[p]
        block = pl.ds(first, 2 * rows)
        pltpu.make_async_copy(out.at[block, :], out_hbm.at[block, :], sems.at[0]).start()

    loop(groups // 2, hand_out)
    for p in range(2):
        level[p] = (jnp.log(totals[p] * (1.0 / bins)) * (1.0 / groups))[0, 0]
    level_copy = pltpu.make_async_copy(level, level_hbm, sems.at[1])
    level_copy.start()
    pltpu.make_async_copy(out, out_hbm, sems.at[0]).wait()
    level_copy.wait()


def body(bins, groups, freqs, zs, emission, step_weights, template_ids):
    templates = emission.shape[1]
    here = emission.shape[2]
    total_rows = here // LANES
    all_rows = templates * total_rows
    rows = all_rows // groups
    xs = freqs // zs
    f32 = jnp.float32
    dma = pltpu.SemaphoreType.DMA
    lines = emission.reshape(templates, total_rows, LANES).transpose(1, 0, 2).reshape(all_rows, LANES)
    hbm = pl.BlockSpec(memory_space=pltpu.HBM)
    vmem = pl.BlockSpec(memory_space=pltpu.VMEM)
    home, total = pl.pallas_call(
        functools.partial(kernel, groups, freqs, zs, bins),
        out_shape=(
            jax.ShapeDtypeStruct((groups, rows, LANES), f32),
            jax.ShapeDtypeStruct((templates, LANES), f32),
        ),
        in_specs=[hbm, hbm, hbm],
        out_specs=(vmem, vmem),
        scratch_shapes=[
            pltpu.VMEM((all_rows, LANES), emission.dtype),
            pltpu.VMEM((all_rows, LANES), f32),
            pltpu.VMEM((step_weights.shape[1], step_weights.shape[0]), f32),
            pltpu.SMEM(template_ids.shape, jnp.int32),
            pltpu.VMEM((groups, rows + 1, LANES), f32),
            pltpu.VMEM((groups, rows + 1, LANES), f32),
            pltpu.VMEM((groups, 1, LANES), f32),
            pltpu.VMEM((2, 2, 1, LANES), f32),
            pltpu.VMEM((2, 2, 1, LANES), f32),
            pltpu.VMEM((groups, rows, LANES), f32),
            pltpu.VMEM((1, LANES), f32),
            pltpu.VMEM((groups // 2, 1, LANES), f32),
            pltpu.VMEM((1, LANES), f32),
            pltpu.VMEM((zs, 1, LANES), f32),
            pltpu.VMEM((1, LANES), f32),
            pltpu.VMEM((2 * xs, 1, LANES), f32),
            dma((3,)), dma((1,)), dma((1,)), dma((2,)), dma((2,)), dma((2, 2)), dma((1,)), dma((1,)), dma((1,)),
            dma((1,)), dma((1,)), dma((1,)), dma((1,)), dma((1,)), dma((1,)), dma((2,)),
        ],
        compiler_params=pltpu.CompilerParams(
            collective_id=0, has_side_effects=True, vmem_limit_bytes=32 * 1024 * 1024
        ),
    )(*(pltpu.with_memory_space_constraint(v, pltpu.HBM) for v in (lines, step_weights.T, template_ids)))
    anywhere = pl.BlockSpec(memory_space=pl.ANY)
    post, level = pl.pallas_call(
        functools.partial(finish, bins),
        out_shape=(
            jax.ShapeDtypeStruct((all_rows, LANES), f32),
            jax.ShapeDtypeStruct((templates,), f32),
        ),
        in_specs=[vmem, vmem],
        out_specs=(anywhere, anywhere),
        scratch_shapes=[pltpu.VMEM((all_rows, LANES), f32), pltpu.SMEM((templates,), f32), dma((2,))],
        compiler_params=pltpu.CompilerParams(vmem_limit_bytes=4 * 1024 * 1024),
    )(home, total)
    posterior = post.reshape(total_rows, templates, LANES).transpose(1, 0, 2).reshape(1, templates, here)
    return posterior, level


def solution(mesh):
    groups, freqs = mesh.shape["tm"], mesh.shape["freq"]
    zs = min(Z_CHIPS, freqs // 2)

    def whole(emission, step_weights, template_ids):
        return jax.shard_map(
            functools.partial(body, emission.shape[2], groups, freqs, zs),
            mesh=mesh,
            in_specs=(P("tm", None, "freq"), P(), P()),
            out_specs=(P("tm", None, "freq"), P()),
            check_vma=False,
        )(emission, step_weights, template_ids)

    return whole
```

```python
import functools

import jax
import jax.numpy as jnp
from jax import lax
from jax.experimental import pallas as pl
from jax.experimental.pallas import tpu as pltpu
from jax.sharding import PartitionSpec as P

MESH = pl.DeviceIdType.MESH
Z_CHIPS = 8
LANES = 128
TAIL = 8
SPARE = 8


def ring_order(chips):
    steps = [chips // 2]
    for d in range(chips // 2 - 1, 0, -1):
        steps += [-d, d]
    return [(d, c) for d in steps for c in (0, 1)] + [(0, 1)]


def loop(count, step):
    lax.fori_loop(0, count, lambda i, c: (step(i), c)[1], 0)


def kernel(groups, freqs, zs, bins, x_hbm, w_hbm, ids_hbm, home, total_ref,
           x_half, x_full, w_ref, ids_ref, stage, recv, halo, edge, beside, work,
           part, part_in, z_part, z_in, x_part, x_in,
           load_sem, send_sem, recv_sem, edge_send, edge_recv, halo_send, halo_recv, back_send, back_recv,
           part_send, part_recv, z_send, z_recv, x_send, x_recv, own_sem):
    part, z_part, x_part = part.at[0], z_part.at[0], x_part.at[0]
    xs = freqs // zs
    chips = groups // 2
    tm = lax.axis_index("tm")
    fq = lax.axis_index("freq")
    yi = tm // 2
    core = lax.rem(tm, 2)
    xi = fq // zs
    zi = lax.rem(fq, zs)
    next_fq = lax.rem(fq + 1, freqs)
    prev_fq = lax.rem(fq + freqs - 1, freqs)
    all_rows = x_hbm.shape[0]
    rows = all_rows // groups
    last = groups - 1
    order = ring_order(chips)

    def member(k):
        return lax.rem(yi + k[0] + chips, chips) * 2 + lax.rem(core + k[1], 2)

    loads = [pltpu.make_async_copy(src, dst, load_sem.at[i])
             for i, (src, dst) in enumerate(((x_hbm, x_half), (w_hbm, w_ref), (ids_hbm, ids_ref)))]
    for copy in loads:
        copy.start()

    barrier = pltpu.get_barrier_semaphore()

    def greet(t, f):
        pl.semaphore_signal(barrier, inc=1, device_id=(t, f), device_id_type=MESH)

    def across_x(k):
        place = lax.rem(xi * 2 + core + k, 2 * xs)
        return place, (yi * 2 + lax.rem(place, 2), place // 2 * zs + zi)

    peers = [(min(abs(k[0]), chips - abs(k[0])), member(k), fq) for k in order]
    peers += [(min(k, zs - k), tm, xi * zs + lax.rem(zi + k, zs)) for k in range(1, zs)]
    peers += [(min(k // 2, xs - k // 2), *across_x(k)[1]) for k in range(1, 2 * xs)]
    for _, t, f in sorted(peers, key=lambda peer: -peer[0]):
        greet(t, f)
    has_next = fq < freqs - 1
    has_prev = fq > 0
    next_turns = has_next & (zi == zs - 1)
    prev_turns = has_prev & (zi == 0)
    low_halo = (yi == 0) & has_prev
    high_halo = (yi == chips - 1) & has_next

    @pl.when(next_turns)
    def _():
        greet(tm, next_fq)

    @pl.when(prev_turns)
    def _():
        greet(tm, prev_fq)

    loads[0].wait()
    low_lanes = lax.broadcasted_iota(jnp.int32, (1, LANES), 1) < LANES // 2

    def widen(o):
        block = pl.ds(pl.multiple_of(o * 2 * rows, 2 * rows), 2 * rows)
        x_full[block, :] = x_half[block, :].astype(jnp.float32)

    def stage_one(o):
        for p in range(2):
            first = o * 2 * rows + p
            for r in range(0, rows, 8):
                stage[2 * o + p, r:r + 8, :] = x_full[pl.ds(first + 2 * r, 8, stride=2), :]
            high = x_full[pl.ds(jnp.minimum(first + 2 * rows, all_rows - 2 + p), 1), :]
            low = x_full[pl.ds(jnp.maximum(first - 2, p), 1), :]
            stage[2 * o + p, rows:rows + 1, :] = jnp.where(
                low_lanes, jnp.where(o < chips - 1, high, 0.0), jnp.where(o > 0, low, 0.0))

    loop(chips, widen)
    loop(chips, stage_one)
    for p in range(2):
        edge[0, p] = x_full[all_rows - 2 + p:all_rows - 1 + p, :]
        edge[1, p] = x_full[p:p + 1, :]

    expected = (groups - 1) + (zs - 1) + (2 * xs - 1)
    pl.semaphore_wait(barrier, expected + next_turns.astype(jnp.int32) + prev_turns.astype(jnp.int32))

    def remote(src, dst, s_sem, r_sem, to):
        return pltpu.make_async_remote_copy(
            src_ref=src, dst_ref=dst, send_sem=s_sem, recv_sem=r_sem, device_id=to, device_id_type=MESH)

    def all_of(ref, count, sem):
        block = ref.at[pl.ds(0, count)]
        pltpu.make_async_copy(block, block, sem).wait()

    def out_copy(k):
        to = member(k)
        return remote(stage.at[to], recv.at[tm], send_sem.at[0], recv_sem.at[0], (to, fq))

    def edge_copy(side, to):
        return remote(edge.at[side], beside.at[side], edge_send.at[side], edge_recv.at[side], (tm, to))

    def halo_copy(side, p):
        owner = p if side == 0 else last - 1 + p
        to = jnp.where(tm == owner, owner + 1 - 2 * p, owner)
        return tm == owner, remote(
            beside.at[side, p], halo.at[tm], halo_send.at[side, p], halo_recv.at[0], (to, fq))

    def halo_pass(side):
        edge_copy(side, fq).wait_recv()
        for p in range(2):
            here, copy = halo_copy(side, p)

            @pl.when(here)
            def _():
                pltpu.make_async_copy(beside.at[side, p], halo.at[tm], halo_recv.at[0]).start()

            @pl.when(jnp.logical_not(here))
            def _():
                copy.start()

    def halo_sent(side):
        for p in range(2):
            here, copy = halo_copy(side, p)

            @pl.when(jnp.logical_not(here))
            def _():
                copy.wait_send()

    @pl.when(has_next)
    def _():
        edge_copy(0, next_fq).start()

    @pl.when(has_prev)
    def _():
        edge_copy(1, prev_fq).start()

    for k in order:
        out_copy(k).start()

    @pl.when(has_prev)
    def _():
        halo_pass(0)

    @pl.when(has_next)
    def _():
        halo_pass(1)

    own = pltpu.make_async_copy(stage.at[tm], recv.at[tm], own_sem.at[0])
    own.start()

    loads[1].wait()
    loads[2].wait()
    slot = lax.broadcasted_iota(jnp.int32, w_ref.shape, 1)
    weights = jnp.sum(jnp.where(slot == ids_ref[core], w_ref[...], 0.0), axis=1, keepdims=True)
    weights = weights / jnp.sum(weights, axis=0, keepdims=True)
    field = (rows + TAIL, LANES)
    staying, rising, falling = (jnp.broadcast_to(weights[i:i + 1, :], field) for i in range(3))
    lane = lax.broadcasted_iota(jnp.int32, field, 1)
    row_index = lax.broadcasted_iota(jnp.int32, field, 0)

    from_other = (high_halo & low_lanes) | (low_halo & jnp.logical_not(low_lanes))

    def emission_of(t):
        tail = jnp.where(from_other, halo[t], recv[t, rows:rows + 1, :])
        return jnp.concatenate([recv[t, 0:rows, :], jnp.broadcast_to(tail, (TAIL, LANES))], axis=0)

    def below(v):
        turned = pltpu.roll(v, 1, 1)
        return jnp.where(lane == 0, pltpu.roll(turned, 1, 0), turned)

    def above(v):
        turned = pltpu.roll(v, LANES - 1, 1)
        return jnp.where(lane == LANES - 1, pltpu.roll(turned, field[0] - 1, 0), turned)

    own.wait()
    all_of(recv, groups - 1, recv_sem.at[0])

    @pl.when(low_halo | high_halo)
    def _():
        all_of(halo, groups, halo_recv.at[0])

    world_low = (yi == 0) & (fq == 0)
    world_high = (yi == chips - 1) & (fq == freqs - 1)
    outside = ((row_index == rows) & world_high) | ((row_index > rows) & world_low)
    b = jnp.ones(field, jnp.float32)
    u = jnp.where(outside, 0.0, b)

    def forward(t, u):
        return emission_of(t) * (staying * u + rising * below(u) + falling * above(u))

    def backward(s, b):
        g = emission_of(s + 1) * b
        return staying * g + rising * above(g) + falling * below(g)

    half = groups // 2

    def early(step, fields):
        u, b = fields
        u = forward(step, u)
        b = backward(last - 1 - step, b)
        work[step] = u[:rows]
        work[last - 1 - step] = b[:rows]
        return u, b

    work[last] = b[:rows]
    u, b = lax.fori_loop(0, half - 1, early, (u, b))
    u = forward(half - 1, u)
    b = backward(half - 1, b)
    middle = u[:rows] * b[:rows]
    work[half - 1] = middle
    part[...] = jnp.sum(middle, axis=0, keepdims=True)

    def spread(src, dst, to_of, mine, count, s_sem, r_sem):
        for k in range(1, count):
            remote(src, dst.at[mine], s_sem.at[0], r_sem.at[0], to_of(k)).start()

    def tree_sum(values):
        while len(values) > 1:
            values = [sum(values[i:i + 2]) for i in range(0, len(values), 2)]
        return values[0]

    def gather(src, dst, to_of, mine, count, s_sem, r_sem):
        dst[mine] = src[...]
        all_of(dst, count - 1, r_sem.at[0])

    y_ring = (lambda k: (lax.rem(yi + k, chips) * 2 + core, fq), yi, chips, part_send, part_recv)
    z_ring = (lambda k: (tm, xi * zs + lax.rem(zi + k, zs)), zi, zs, z_send, z_recv)
    x_ring = (lambda k: across_x(k)[1], xi * 2 + core, 2 * xs, x_send, x_recv)
    spread(part, part_in, *y_ring)

    def late(step, fields):
        u, b = fields
        u = forward(step, u)
        b = backward(last - 1 - step, b)
        work[step] = u[:rows] * work[step]
        work[last - 1 - step] = work[last - 1 - step] * b[:rows]
        return u, b

    u, _ = lax.fori_loop(half, last, late, (u, b))
    work[last] = forward(last, u)[:rows] * work[last]

    def back_copy(k):
        to = member(k)
        return remote(work.at[to], home.at[tm], back_send.at[0], back_recv.at[0], (to, fq))

    own_back = pltpu.make_async_copy(work.at[tm], home.at[tm], own_sem.at[1])
    own_back.start()
    for k in order[:len(order) // 2]:
        back_copy(k).start()

    gather(part, part_in, *y_ring)
    z_part[...] = tree_sum([part_in[i] for i in range(chips)])
    spread(z_part, z_in, *z_ring)
    for k in order[len(order) // 2:]:
        back_copy(k).start()
    all_of(stage, groups - 1, send_sem.at[0])

    gather(z_part, z_in, *z_ring)
    x_part[...] = tree_sum([z_in[i] for i in range(zs)])
    spread(x_part, x_in, *x_ring)

    @pl.when(has_next)
    def _():
        edge_copy(0, next_fq).wait_send()
        halo_sent(1)

    @pl.when(has_prev)
    def _():
        edge_copy(1, prev_fq).wait_send()
        halo_sent(0)

    all_of(part_in, chips - 1, part_send.at[0])
    all_of(z_in, zs - 1, z_send.at[0])
    gather(x_part, x_in, *x_ring)
    for p in range(2):
        whole = jnp.sum(tree_sum([x_in[2 * i + p] for i in range(xs)]), axis=1, keepdims=True)
        total_ref[p:p + 1, :] = jnp.broadcast_to(whole, (1, LANES))

    own_back.wait()
    all_of(home, groups - 1, back_recv.at[0])
    all_of(x_in, 2 * xs - 1, x_send.at[0])
    all_of(work, groups - 1, back_send.at[0])


def finish(bins, home, total_ref, out_hbm, level_hbm, out, level, sems):
    groups, rows = home.shape[0], home.shape[1]
    totals = [total_ref[p:p + 1, :] for p in range(2)]
    scales = [bins / total for total in totals]

    def hand_out(o):
        first = pl.multiple_of(o * 2 * rows, 2 * rows)
        for p in range(2):
            for r in range(0, rows, 8):
                out[pl.ds(first + p + 2 * r, 8, stride=2), :] = home[2 * o + p, r:r + 8, :] * scales[p]
        block = pl.ds(first, 2 * rows)
        pltpu.make_async_copy(out.at[block, :], out_hbm.at[block, :], sems.at[0]).start()

    loop(groups // 2, hand_out)
    for p in range(2):
        level[p] = (jnp.log(totals[p] * (1.0 / bins)) * (1.0 / groups))[0, 0]
    level_copy = pltpu.make_async_copy(level, level_hbm, sems.at[1])
    level_copy.start()
    pltpu.make_async_copy(out, out_hbm, sems.at[0]).wait()
    level_copy.wait()


def body(bins, groups, freqs, zs, emission, step_weights, template_ids):
    templates = emission.shape[1]
    here = emission.shape[2]
    total_rows = here // LANES
    all_rows = templates * total_rows
    rows = all_rows // groups
    xs = freqs // zs
    f32 = jnp.float32
    dma = pltpu.SemaphoreType.DMA
    lines = emission.reshape(templates, total_rows, LANES).transpose(1, 0, 2).reshape(all_rows, LANES)
    hbm = pl.BlockSpec(memory_space=pltpu.HBM)
    vmem = pl.BlockSpec(memory_space=pltpu.VMEM)
    home, total = pl.pallas_call(
        functools.partial(kernel, groups, freqs, zs, bins),
        out_shape=(
            jax.ShapeDtypeStruct((groups, rows, LANES), f32),
            jax.ShapeDtypeStruct((TAIL, LANES), f32),
        ),
        in_specs=[hbm, hbm, hbm],
        out_specs=(vmem, vmem),
        scratch_shapes=[
            pltpu.VMEM((all_rows, LANES), emission.dtype),
            pltpu.VMEM((all_rows, LANES), f32),
            pltpu.VMEM((step_weights.shape[1], step_weights.shape[0]), f32),
            pltpu.SMEM(template_ids.shape, jnp.int32),
            pltpu.VMEM((groups, rows + 1, LANES), f32),
            pltpu.VMEM((groups, rows + 1, LANES), f32),
            pltpu.VMEM((groups + SPARE, 1, LANES), f32),
            pltpu.VMEM((2 + SPARE, 2, 1, LANES), f32),
            pltpu.VMEM((2 + SPARE, 2, 1, LANES), f32),
            pltpu.VMEM((groups, rows, LANES), f32),
            pltpu.VMEM((1 + SPARE, 1, LANES), f32),
            pltpu.VMEM((groups // 2 + SPARE, 1, LANES), f32),
            pltpu.VMEM((1 + SPARE, 1, LANES), f32),
            pltpu.VMEM((zs + SPARE, 1, LANES), f32),
            pltpu.VMEM((1 + SPARE, 1, LANES), f32),
            pltpu.VMEM((2 * xs + SPARE, 1, LANES), f32),
            dma((3,)), dma((1,)), dma((1,)), dma((2,)), dma((2,)), dma((2, 2)), dma((1,)), dma((1,)), dma((1,)),
            dma((1,)), dma((1,)), dma((1,)), dma((1,)), dma((1,)), dma((1,)), dma((2,)),
        ],
        compiler_params=pltpu.CompilerParams(
            collective_id=0, has_side_effects=True, vmem_limit_bytes=32 * 1024 * 1024
        ),
    )(*(pltpu.with_memory_space_constraint(v, pltpu.HBM) for v in (lines, step_weights.T, template_ids)))
    anywhere = pl.BlockSpec(memory_space=pl.ANY)
    post, level = pl.pallas_call(
        functools.partial(finish, bins),
        out_shape=(
            jax.ShapeDtypeStruct((all_rows, LANES), f32),
            jax.ShapeDtypeStruct((templates,), f32),
        ),
        in_specs=[vmem, vmem],
        out_specs=(anywhere, anywhere),
        scratch_shapes=[pltpu.VMEM((all_rows, LANES), f32), pltpu.SMEM((templates,), f32), dma((2,))],
        compiler_params=pltpu.CompilerParams(vmem_limit_bytes=4 * 1024 * 1024),
    )(home, total)
    posterior = post.reshape(total_rows, templates, LANES).transpose(1, 0, 2).reshape(1, templates, here)
    return posterior, level


def solution(mesh):
    groups, freqs = mesh.shape["tm"], mesh.shape["freq"]
    zs = min(Z_CHIPS, freqs // 2)

    def whole(emission, step_weights, template_ids):
        return jax.shard_map(
            functools.partial(body, emission.shape[2], groups, freqs, zs),
            mesh=mesh,
            in_specs=(P("tm", None, "freq"), P(), P()),
            out_specs=(P("tm", None, "freq"), P()),
            check_vma=False,
        )(emission, step_weights, template_ids)

    return whole
```
